512 devices in a mesh: lon: 64 (over z_lo, x, core), lat: 8 (over y, z_hi).
Axes of the slice: x: 4, y: 4, z: 16 (z_hi: 2, z_lo: 8; z = z_hi * 8 + z_lo), core: 2. Of those that a mesh axis runs over, the one named last changes fastest.
Arguments:
- state: bfloat16 [256, 1024, 192], P('lat', 'lon'), may hold values from -6 to 6
- land_mask: int32 [256, 1024], P('lat', 'lon'), may hold values 0 or 1
- cotangent: bfloat16 [256, 1024, 192], P('lat', 'lon'), may hold values from -6 to 6
- kernel: bfloat16 [7, 7, 192], replicated, may hold values from -0.875 to 0.875
- norm_gain: float32 [192], replicated, may hold values from 0.5 to 2
- norm_bias: float32 [192], replicated, may hold values from -3 to 3
- weight_in: bfloat16 [192, 768], replicated, may hold values from -0.4375 to 0.4375
- bias_hidden: float32 [768], replicated, may hold values from -3 to 3
- weight_out: bfloat16 [768, 192], replicated, may hold values from -0.21875 to 0.21875
- bias_out: float32 [192], replicated, may hold values from -3 to 3
- layer_scale: float32 [192], replicated, may hold values from 0.3 to 1.5
Outputs:
- block_out: bfloat16 [256, 1024, 192], P('lat', 'lon')
- grad_state: bfloat16 [256, 1024, 192], P('lat', 'lon')
- grad_kernel: float32 [7, 7, 192], replicated
- grad_norm_gain: float32 [192], replicated
- grad_norm_bias: float32 [192], replicated
- grad_weight_in: float32 [192, 768], replicated
- grad_bias_hidden: float32 [768], replicated
- grad_weight_out: float32 [768, 192], replicated
- grad_bias_out: float32 [192], replicated
- grad_layer_scale: float32 [192], replicated
The draws below stay inside these ranges and needn't reach their ends.
All inputs are finite; a program needn't handle non-finite values. No bound on the sum of `land_mask` on one device may be relied on, other than what follows from the above.
Results may differ from the reference program's by a relative error of at most 0.0069.
Values may be sent and summed in bfloat16 or wider, within the bound.
A program may use at most 64 MiB of HBM per device.

```python
import math
import jax
import jax.numpy as jnp
from jax import lax

C = 192
HID = 768
CLAT = 32
NLAT = 256
NLON = 1024
N_LAT = 8


def plant(entries, key, low, high):
    extent = entries.shape
    place = [jax.random.randint(jax.random.fold_in(key, axis), (), 0, extent[axis]) for axis in range(len(extent))]
    entries = entries.at[tuple(place)].set(low)
    longest = extent.index(max(extent))
    place[longest] = (place[longest] + 1) % extent[longest]
    return entries.at[tuple(place)].set(high)


def steps_of(stream_key, dims, shards, low, largest):
    gain = 1.0
    for position, parts in shards:
        heights = jax.random.uniform(jax.random.fold_in(jax.random.fold_in(stream_key, 6), position), (parts,), jnp.float32, low / len(shards), largest / len(shards))
        gain = gain * jnp.repeat(jnp.exp(heights), dims[position] // parts).reshape((-1,) + (1,) * (len(dims) - 1 - position))
    return gain


def normal_values(stream_key, dims, spread, most, split=(), held_as=jnp.bfloat16):
    drawn = spread * jax.random.normal(stream_key, dims, jnp.float32)
    if split:
        drawn = drawn * steps_of(stream_key, dims, split, -0.22, 0.18)
    return jnp.clip(drawn, -most, most).astype(held_as)


def setup_inputs(seed: int = 0) -> dict:
    splits = jax.random.split(jax.random.key(seed), 12)
    return {
        "state": normal_values(splits[0], (NLAT, NLON, C), 1.0, 6.0, ((0, 8), (1, 64))),
        "land_mask": plant((jax.random.randint(splits[1], (NLAT, NLON), 0, 4) < 3).astype(jnp.int32), jax.random.fold_in(splits[1], 1), 0, 1),
        "cotangent": normal_values(splits[2], (NLAT, NLON, C), 1.0, 6.0, ((0, 8), (1, 64))),
        "kernel": normal_values(splits[3], (7, 7, C), 49 ** -0.5, 0.875),
        "norm_gain": jnp.clip(jnp.exp(jax.random.uniform(splits[4], (C,), jnp.float32, math.log(0.5), math.log(2.0))), 0.5, 2.0),
        "norm_bias": normal_values(splits[5], (C,), 0.5, 3.0, (), jnp.float32),
        "weight_in": normal_values(splits[6], (C, HID), C ** -0.5, 0.4375),
        "bias_hidden": normal_values(splits[7], (HID,), 0.5, 3.0, (), jnp.float32),
        "weight_out": normal_values(splits[8], (HID, C), HID ** -0.5, 0.21875),
        "bias_out": normal_values(splits[9], (C,), 0.5, 3.0, (), jnp.float32),
        "layer_scale": jnp.clip(jnp.exp(jax.random.uniform(splits[10], (C,), jnp.float32, math.log(0.3), math.log(1.5))), 0.3, 1.5),
    }


EPSILON = 1e-06

def depthwise(padded, kernel, row_count, col_count):
    running = jnp.zeros((row_count, col_count, padded.shape[2]), jnp.float32)
    for tap_row in range(7):
        for tap_col in range(7):
            window = padded[tap_row:tap_row + row_count, tap_col:tap_col + col_count].astype(jnp.float32)
            running = running + window * kernel[tap_row, tap_col].astype(jnp.float32)
    return running

def kernel_grad(padded, mixed_cot, row_count, col_count):
    cot_float = mixed_cot.astype(jnp.float32)
    pieces = []
    for tap_row in range(7):
        for tap_col in range(7):
            window = padded[tap_row:tap_row + row_count, tap_col:tap_col + col_count].astype(jnp.float32)
            pieces.append(lax.optimization_barrier(jnp.sum(window * cot_float, axis=(0, 1))))
    return jnp.stack(pieces).reshape(7, 7, padded.shape[2])

def outer_sum(left, right):
    return lax.dot_general(left, right, (((0,), (0,)), ((), ())), preferred_element_type=jnp.float32)

def gelu_tanh(values):
    return jax.nn.gelu(values, approximate=True)

def cell_pass(padded, state, land_cells, cotangent, kernel, norm_gain, norm_bias, weight_in, bias_hidden, weight_out, bias_out, layer_scale):
    row_count, col_count, channels = state.shape
    mixed = depthwise(padded, kernel, row_count, col_count)
    average = lax.optimization_barrier(jnp.mean(mixed, axis=2, keepdims=True))
    centred = mixed - average
    variance = lax.optimization_barrier(jnp.mean(centred * centred, axis=2, keepdims=True))
    inv_std = lax.rsqrt(variance + EPSILON)
    unit_mixed = (centred * inv_std).reshape(-1, channels)
    flat_inv = inv_std.reshape(-1, 1)
    normed = (unit_mixed * norm_gain + norm_bias).astype(jnp.bfloat16)
    pre_act = jnp.dot(normed, weight_in, preferred_element_type=jnp.float32) + bias_hidden
    hidden = gelu_tanh(pre_act).astype(jnp.bfloat16)
    branch = jnp.dot(hidden, weight_out, preferred_element_type=jnp.float32) + bias_out
    sea_weight = land_cells.astype(jnp.float32).reshape(-1, 1)
    flat_state = state.reshape(-1, channels).astype(jnp.float32)
    flat_cot = cotangent.reshape(-1, channels).astype(jnp.float32)
    result = (sea_weight * (flat_state + layer_scale * branch)).astype(jnp.bfloat16)
    grad_branch = sea_weight * layer_scale * flat_cot
    branch_cot = grad_branch.astype(jnp.bfloat16)
    grad_hidden = jnp.dot(branch_cot, weight_out.T, preferred_element_type=jnp.float32)
    unused, pullback = jax.vjp(gelu_tanh, pre_act)
    grad_pre = pullback(grad_hidden)[0]
    pre_cot = grad_pre.astype(jnp.bfloat16)
    grad_normed = jnp.dot(pre_cot, weight_in.T, preferred_element_type=jnp.float32)
    grad_unit = grad_normed * norm_gain
    grad_mixed = flat_inv * (grad_unit - lax.optimization_barrier(jnp.mean(grad_unit, axis=1, keepdims=True)) - unit_mixed * lax.optimization_barrier(jnp.mean(grad_unit * unit_mixed, axis=1, keepdims=True)))
    mixed_cot = grad_mixed.astype(jnp.bfloat16).reshape(row_count, col_count, channels)
    partials = (kernel_grad(padded, mixed_cot, row_count, col_count), lax.optimization_barrier(jnp.sum(grad_normed * unit_mixed, axis=0)), lax.optimization_barrier(jnp.sum(grad_normed, axis=0)), outer_sum(normed, pre_cot), lax.optimization_barrier(jnp.sum(grad_pre, axis=0)), outer_sum(hidden, branch_cot), lax.optimization_barrier(jnp.sum(grad_branch, axis=0)), lax.optimization_barrier(jnp.sum(sea_weight * flat_cot * branch, axis=0)))
    return (result.reshape(row_count, col_count, channels), mixed_cot, partials)

def extend(field):
    lon_wide = jnp.concatenate([field[:, -3:], field, field[:, :3]], axis=1)
    south = jnp.zeros((3,) + lon_wide.shape[1:], field.dtype)
    fold_rows = lon_wide[-3:][::-1, ::-1]
    return (south, lon_wide, fold_rows)

def reference(state, land_mask, cotangent, kernel, norm_gain, norm_bias, weight_in, bias_hidden, weight_out, bias_out, layer_scale):
    channels = state.shape[2]
    masked = state * land_mask[:, :, None].astype(state.dtype)
    south, lon_wide, fold_rows = extend(masked)
    padded = jnp.concatenate([south, lon_wide, fold_rows], axis=0)

    def advance(running, block_index):
        row_start = (block_index * CLAT).astype(jnp.int32)
        pad_block = lax.dynamic_slice_in_dim(padded, row_start, CLAT + 6, 0)
        state_block = lax.dynamic_slice_in_dim(state, row_start, CLAT, 0)
        mask_block = lax.dynamic_slice_in_dim(land_mask, row_start, CLAT, 0)
        cot_block = lax.dynamic_slice_in_dim(cotangent, row_start, CLAT, 0)
        result, mixed_cot, partials = cell_pass(pad_block, state_block, mask_block, cot_block, kernel, norm_gain, norm_bias, weight_in, bias_hidden, weight_out, bias_out, layer_scale)
        running = tuple((acc + part for acc, part in zip(running, partials)))
        return (running, (result, mixed_cot))
    start_sums = (jnp.zeros((7, 7, channels), jnp.float32), jnp.zeros((channels,), jnp.float32), jnp.zeros((channels,), jnp.float32), jnp.zeros((channels, HID), jnp.float32), jnp.zeros((HID,), jnp.float32), jnp.zeros((HID, channels), jnp.float32), jnp.zeros((channels,), jnp.float32), jnp.zeros((channels,), jnp.float32))
    summed, (results, cots) = lax.scan(advance, start_sums, jnp.arange(N_LAT, dtype=jnp.int32))
    block_out = results.reshape(NLAT, NLON, channels)
    mixed_cot = cots.reshape(NLAT, NLON, channels)
    south_cot, lon_cot, fold_cot = extend(mixed_cot)
    inner = jnp.concatenate([south_cot, lon_cot, jnp.zeros_like(fold_cot)], axis=0)
    flipped = kernel[::-1, ::-1]

    def backward(carry_unused, block_index):
        row_start = (block_index * CLAT).astype(jnp.int32)
        inner_block = lax.dynamic_slice_in_dim(inner, row_start, CLAT + 6, 0)
        return (carry_unused, depthwise(inner_block, flipped, CLAT, NLON))
    unused, grad_blocks = lax.scan(backward, jnp.zeros((), jnp.float32), jnp.arange(N_LAT, dtype=jnp.int32))
    grad_masked = grad_blocks.reshape(NLAT, NLON, channels)
    zero_rows = jnp.zeros((6,) + fold_cot.shape[1:], fold_cot.dtype)
    fold_part = depthwise(jnp.concatenate([zero_rows, fold_cot], axis=0), kernel, 3, NLON)
    grad_masked = grad_masked.at[NLAT - 3:].add(fold_part)
    sea_weight = land_mask[:, :, None].astype(jnp.float32)
    grad_state = (sea_weight * (cotangent.astype(jnp.float32) + grad_masked)).astype(jnp.bfloat16)
    factor = 1.0 / math.sqrt(NLAT * NLON)
    scaled = tuple((part * factor for part in summed))
    return (block_out, grad_state, scaled[0], scaled[1], scaled[2], scaled[3], scaled[4], scaled[5], scaled[6], scaled[7])
```

```python
import functools
import math

import jax
import jax.numpy as jnp
from jax import lax
from jax.experimental import pallas as pl
from jax.experimental.pallas import tpu as pltpu
from jax.sharding import PartitionSpec as P

EPSILON = 1e-06
MESH = pl.DeviceIdType.MESH
F32 = jnp.float32
BF16 = jnp.bfloat16

ROWS, COLS, C, HID = 32, 16, 192, 768
CELLS = ROWS * COLS
PADR, WIDE = ROWS + 6, 32
WROWS = C * HID // 128
SROWS = 64
TOT = WROWS + 2 * SROWS
GELU_A = math.sqrt(2.0 / math.pi)
GELU_B = 0.044715


def groups(nlon, nlat):
    px = 4 if nlon >= 64 else 2
    nzl = nlon // (2 * px)
    nzh = 2 if nlat >= 8 else 1
    return px, nzl, nzh, nlat // nzh


def one_hot(shape, pick):
    a = lax.broadcasted_iota(jnp.int32, shape, 0)
    b = lax.broadcasted_iota(jnp.int32, shape, 1)
    return pick(a, b).astype(F32).astype(BF16)


def dot(a, b, contract=((1,), (0,))):
    return lax.dot_general(a, b, (contract, ((), ())), preferred_element_type=F32)


def main_kernel(
    nlon,
    nlat,
    state,
    mask,
    cot,
    kern,
    gain,
    nbias,
    w_in,
    b_hid,
    w_out,
    b_out,
    scale,
    block_out,
    grad_state,
    total,
    pad,
    shifted,
    padq,
    shiftq,
    taps,
    maskb,
    normed_s,
    precot_s,
    hidden_s,
    bcot_s,
    mcot_s,
    sums,
    sumh,
    small,
    csend,
    crecv,
    rsend,
    rrecv,
    wbuf,
    wrecv,
    psum,
    pay,
    xrecv,
    zacc,
    zrecv,
    ztot,
    abuf,
    fin,
    col_s,
    col_r,
    row_s,
    row_r,
    core_s,
    core_r,
    xs,
    xr,
    zs,
    zr,
    zas,
    zar,
    xas,
    xar,
):
    px, nzl, nzh, py = groups(nlon, nlat)
    nplane, nz = px * py, nzl * nzh
    chunk = TOT // nplane
    zrows = max(8, -(-chunk // nz // 8) * 8)
    if zrows * nz < chunk:
        zrows += 8
    owners = chunk // zrows

    lon = lax.axis_index("lon")
    lat = lax.axis_index("lat")
    core = lon % 2
    x = (lon // 2) % px
    zl = lon // (2 * px)
    zh = lat % nzh
    y = lat // nzh
    plane = y * px + x
    zi = zh * nzl + zl
    is_top = lat == nlat - 1
    has_south = lat > 0

    def device(la, lo):
        return {"lon": lo, "lat": la}

    east = device(lat, (lon + 1) % nlon)
    west = device(lat, (lon + nlon - 1) % nlon)
    north = device(
        jnp.where(is_top, lat, (lat + 1) % nlat), jnp.where(is_top, nlon - 1 - lon, lon)
    )
    south = device((lat + nlat - 1) % nlat, lon)
    pair = device(lat, lon + 1 - 2 * core)

    def in_plane(k):
        return device((k // px) * nzh + zh, zl * (2 * px) + (k % px) * 2 + core)

    def in_z(k):
        return device(y * nzh + k // nzl, (k % nzl) * (2 * px) + x * 2 + core)

    barrier = pltpu.get_barrier_semaphore()

    def hello(target):
        pl.semaphore_signal(barrier, inc=1, device_id=target, device_id_type=MESH)

    hello(east)
    hello(west)
    hello(north)
    hello(pair)

    @pl.when(has_south)
    def _():
        hello(south)

    @pl.loop(1, nplane)
    def _(d):
        hello(in_plane((plane + d) % nplane))

    @pl.loop(1, nz)
    def _(d):
        hello(in_z((zi + d) % nz))

    for a in range(7):
        k7 = kern[a].astype(F32)
        for b in range(7):
            taps[a * 7 + b] = jnp.broadcast_to(k7[b : b + 1], (8, C))
    sums[...] = jnp.zeros_like(sums)
    sumh[...] = jnp.zeros_like(sumh)
    small[...] = jnp.zeros_like(small)
    by_row = one_hot((CELLS, ROWS), lambda a, b: a // COLS == b)
    by_col = one_hot((CELLS, COLS), lambda a, b: a % COLS == b).astype(F32)
    sea = dot(by_row, mask[...].astype(F32).astype(BF16), ((1,), (1,))) * by_col
    maskb[...] = dot(sea.astype(BF16), jnp.ones((COLS, C), BF16)).reshape(ROWS, COLS, C)
    own = (state[...].astype(F32) * maskb[...]).reshape(ROWS, COLS, C)
    pad[3 : 3 + ROWS, 8:24, :] = own

    east_pick = one_hot((96, CELLS), lambda a, b: (a // 3) * COLS + 13 + a % 3 == b)
    west_pick = one_hot((96, CELLS), lambda a, b: (a // 3) * COLS + a % 3 == b)
    left_put = one_hot(
        (ROWS * 8, 96), lambda a, b: (a % 8 >= 5) & ((a // 8) * 3 + a % 8 - 5 == b)
    )
    right_put = one_hot((ROWS * 8, 96), lambda a, b: (a % 8 < 3) & ((a // 8) * 3 + a % 8 == b))

    def send_columns(n, cells):
        csend[n, 0] = dot(east_pick, cells).astype(BF16)
        csend[n, 1] = dot(west_pick, cells).astype(BF16)
        copies = [
            pltpu.make_async_remote_copy(
                src_ref=csend.at[n, i],
                dst_ref=crecv.at[n, i],
                send_sem=col_s.at[n, i],
                recv_sem=col_r.at[n, i],
                device_id=target,
                device_id_type=MESH,
            )
            for i, target in ((0, east), (1, west))
        ]
        for copy in copies:
            copy.start()
        return copies

    def take_columns(n, copies, field):
        for copy in copies:
            copy.wait()
        field[3 : 3 + ROWS, 0:8, :] = dot(left_put, crecv[n, 0]).reshape(ROWS, 8, C)
        field[3 : 3 + ROWS, 24:32, :] = dot(right_put, crecv[n, 1]).reshape(ROWS, 8, C)

    def send_rows(n, field):
        rsend[n, 0] = field[3:6].astype(BF16)
        rsend[n, 1] = field[ROWS : ROWS + 3].astype(BF16)
        slot = jnp.where(is_top, 0, 1)
        up = pltpu.make_async_remote_copy(
            src_ref=rsend.at[n, 1],
            dst_ref=rrecv.at[n, slot],
            send_sem=row_s.at[n, 1],
            recv_sem=row_r.at[n, slot],
            device_id=north,
            device_id_type=MESH,
        )
        up.start()
        down = pltpu.make_async_remote_copy(
            src_ref=rsend.at[n, 0],
            dst_ref=rrecv.at[n, 0],
            send_sem=row_s.at[n, 0],
            recv_sem=row_r.at[n, 0],
            device_id=south,
            device_id_type=MESH,
        )

        @pl.when(has_south)
        def _():
            down.start()

        return up, down

    def take_rows(n, copies, field):
        up, down = copies
        up.wait_send()
        down.wait_recv()

        @pl.when(has_south)
        def _():
            down.wait_send()
            pltpu.make_async_remote_copy(
                src_ref=rsend.at[n, 1],
                dst_ref=rrecv.at[n, 1],
                send_sem=row_s.at[n, 1],
                recv_sem=row_r.at[n, 1],
                device_id=south,
                device_id_type=MESH,
            ).wait_recv()
            field[0:3] = rrecv[n, 1].astype(F32)

        @pl.when(jnp.logical_not(has_south))
        def _():
            field[0:3] = jnp.zeros((3, WIDE, C), F32)

        @pl.when(is_top)
        def _():
            turn = one_hot((WIDE, WIDE), lambda a, b: a + b == WIDE - 1)
            for m in range(3):
                field[ROWS + 3 + m] = dot(turn, rrecv[n, 0, 2 - m])

        @pl.when(jnp.logical_not(is_top))
        def _():
            field[ROWS + 3 : ROWS + 6] = rrecv[n, 0].astype(F32)

    def shift(field, out):
        @pl.loop(0, PADR)
        def _(r):
            for b in range(7):
                out[b, r] = field[r, 5 + b : 21 + b, :].reshape(2, 8, C)

    def conv_rows(source, r0, rows, flip):
        acc = jnp.zeros((rows, 2, 8, C), F32)
        for b in range(7):
            for a in range(7):
                k = taps[48 - a * 7 - b] if flip else taps[a * 7 + b]
                acc = acc + source[b, pl.ds(r0 + a, rows)] * k
        return acc

    pl.semaphore_wait(
        barrier, 4 + (nplane - 1) + (nz - 1) + jnp.where(has_south, 1, 0)
    )
    own_cells = own.astype(BF16).reshape(CELLS, C)
    copies = send_columns(0, own_cells)
    take_columns(0, copies, pad)
    copies = send_rows(0, pad)
    take_rows(0, copies, pad)
    shift(pad, shifted)

    block = 8
    cells = block * COLS

    @pl.loop(0, ROWS // block)
    def _(blk):
        r0 = blk * block
        here = pl.ds(pl.multiple_of(r0 * COLS, cells), cells)
        mixed = jnp.concatenate(
            [conv_rows(shifted, r0 + 4 * i, 4, False).reshape(4 * COLS, C) for i in range(block // 4)],
            axis=0,
        )
        average = jnp.sum(mixed, axis=1, keepdims=True) * (1.0 / C)
        centred = mixed - average
        variance = jnp.sum(centred * centred, axis=1, keepdims=True) * (1.0 / C)
        inv_std = lax.rsqrt(variance + EPSILON)
        unit = centred * inv_std
        normed = (unit * gain[...] + nbias[...]).astype(BF16)
        normed_s[here, :] = normed
        pre = dot(normed, w_in[...]) + b_hid[...]
        square = pre * pre
        t = jnp.tanh(GELU_A * pre * (1.0 + GELU_B * square))
        half = 0.5 * (1.0 + t)
        hidden = (pre * half).astype(BF16)
        hidden_s[here, :] = hidden
        slope = half + pre * (0.5 * GELU_A) * (1.0 - t * t) * (1.0 + 3.0 * GELU_B * square)
        branch = dot(hidden, w_out[...], ((1,), (1,))) + b_out[...]
        rows_here = pl.ds(r0, block)
        sea_w = maskb[rows_here].reshape(cells, C)
        st = state[rows_here].astype(F32).reshape(cells, C)
        ct = cot[rows_here].astype(F32).reshape(cells, C) * sea_w
        block_out[rows_here] = (
            (sea_w * (st + scale[...] * branch)).astype(BF16).reshape(block, COLS, C)
        )
        grad_branch = ct * scale[...]
        bcot = grad_branch.astype(BF16)
        bcot_s[here, :] = bcot
        grad_pre = dot(bcot, w_out[...]) * slope
        precot = grad_pre.astype(BF16)
        precot_s[here, :] = precot
        grad_normed = dot(precot, w_in[...], ((1,), (1,)))
        grad_unit = grad_normed * gain[...]
        mean_a = jnp.sum(grad_unit, axis=1, keepdims=True) * (1.0 / C)
        mean_b = jnp.sum(grad_unit * unit, axis=1, keepdims=True) * (1.0 / C)
        grad_mixed = inv_std * (grad_unit - mean_a - unit * mean_b)
        mcot = grad_mixed.astype(BF16)
        mcot_s[here, :] = mcot
        padq[pl.ds(3 + r0, block), 8:24, :] = mcot.astype(F32).reshape(block, COLS, C)

        def fold8(v):
            return jnp.sum(v.reshape(cells // 8, 8, v.shape[1]), axis=0)

        sums[0] += fold8(grad_normed * unit)
        sums[1] += fold8(grad_normed)
        sums[2] += fold8(grad_branch)
        sums[3] += fold8(ct * branch)
        sumh[...] += fold8(grad_pre)

    copies = send_columns(1, mcot_s[...])

    for t in range(HID // 256):
        wide = slice(256 * t, 256 * t + 256)
        g_in = dot(normed_s[...], precot_s[:, wide], ((0,), (0,)))
        g_out = dot(bcot_s[...], hidden_s[:, wide], ((0,), (0,)))
        for j in range(2):
            to = slice((2 * t + j) * C, (2 * t + j + 1) * C)
            wbuf[0, to, :] = g_in[:, 128 * j : 128 * j + 128]
            wbuf[1, to, :] = g_out[:, 128 * j : 128 * j + 128]

    def to_pair(i, rows):
        return pltpu.make_async_remote_copy(
            src_ref=wbuf.at[1 - core, rows],
            dst_ref=wrecv.at[rows],
            send_sem=core_s.at[i],
            recv_sem=core_r.at[i],
            device_id=pair,
            device_id_type=MESH,
        )

    pair_w = to_pair(0, pl.ds(0, WROWS))
    pair_w.start()

    take_columns(1, copies, padq)
    copies = send_rows(1, padq)

    for b in range(7):

        def step(i, accs, b=b):
            r0 = i * 4
            m = padq[pl.ds(3 + r0, 4), 8:24, :].reshape(4, 2, 8, C)
            return tuple(
                accs[a] + jnp.sum((m * shifted[b, pl.ds(r0 + a, 4)]).reshape(8, 8, C), axis=0)
                for a in range(7)
            )

        accs = lax.fori_loop(0, ROWS // 4, step, tuple(jnp.zeros((8, C), F32) for _ in range(7)))
        for a in range(7):
            small[a * 7 + b : a * 7 + b + 1, 0:C] = jnp.sum(accs[a], axis=0, keepdims=True)
    for i in range(4):
        small[49 + i : 50 + i, 0:C] = jnp.sum(sums[i], axis=0, keepdims=True)
    hid_row = jnp.sum(sumh[...], axis=0, keepdims=True)
    for i in range(3):
        small[53 + i : 54 + i, :] = hid_row[:, 256 * i : 256 * i + 256]
    wbuf[0, WROWS:, :] = small[:, 0:128]
    wbuf[1, WROWS:, :] = small[:, 128:256]
    pair_s = to_pair(1, pl.ds(WROWS, SROWS))
    pair_s.start()

    take_rows(1, copies, padq)
    pair_w.wait()
    pair_s.wait()

    @pl.loop(0, WROWS // 64)
    def _(i):
        rows = pl.ds(pl.multiple_of(i * 64, 64), 64)
        both = wbuf[core, rows, :] + wrecv[rows, :]
        psum[rows, :] = both
        pay[rows, :] = both.astype(BF16)

    both = wbuf[core, WROWS:, :] + wrecv[WROWS:, :]
    high = both.astype(BF16)
    low = both - high.astype(F32)
    psum[WROWS : WROWS + SROWS, :] = high.astype(F32)
    psum[WROWS + SROWS :, :] = low
    pay[WROWS : WROWS + SROWS, :] = high
    pay[WROWS + SROWS :, :] = low.astype(BF16)

    def rows_of(k, size):
        return pl.ds(pl.multiple_of(k * size, 8), size)

    def plane_copy(k, sender):
        return pltpu.make_async_remote_copy(
            src_ref=pay.at[rows_of(k, chunk)],
            dst_ref=xrecv.at[sender],
            send_sem=xs.at[k],
            recv_sem=xr.at[sender],
            device_id=in_plane(k),
            device_id_type=MESH,
        )

    @pl.loop(1, nplane)
    def _(d):
        plane_copy((plane + d) % nplane, plane).start()

    shift(padq, shiftq)

    @pl.loop(0, ROWS // 4)
    def _(i):
        rows_here = pl.ds(i * 4, 4)
        grad = conv_rows(shiftq, i * 4, 4, True).reshape(4, COLS, C)
        grad_state[rows_here] = (
            maskb[rows_here] * (cot[rows_here].astype(F32) + grad)
        ).astype(BF16)

    @pl.when(is_top)
    def _():
        first = ROWS - 4
        acc = conv_rows(shiftq, first, 4, True)
        parts = [acc[i] for i in range(4)]
        for i in range(1, 4):
            for a in range(7 - i, 7):
                for b in range(7):
                    change = taps[a * 7 + b] - taps[48 - a * 7 - b]
                    parts[i] = parts[i] + shiftq[b, first + i + a] * change
        for i in range(1, 4):
            grad_state[first + i] = (
                maskb[first + i] * (cot[first + i].astype(F32) + parts[i].reshape(COLS, C))
            ).astype(BF16)

    zacc[...] = psum[rows_of(plane, chunk), :]

    @pl.loop(1, nplane)
    def _(d):
        k = (plane + d) % nplane
        copy = plane_copy(k, k)
        copy.wait()
        zacc[...] += xrecv[k].astype(F32)

    def z_copy(k, sender):
        return pltpu.make_async_remote_copy(
            src_ref=zacc.at[rows_of(k, zrows)],
            dst_ref=zrecv.at[sender],
            send_sem=zs.at[k],
            recv_sem=zr.at[sender],
            device_id=in_z(k),
            device_id_type=MESH,
        )

    def z_back(owner, k):
        return pltpu.make_async_remote_copy(
            src_ref=ztot.at[rows_of(owner, zrows)],
            dst_ref=ztot.at[rows_of(owner, zrows)],
            send_sem=zas.at[k],
            recv_sem=zar.at[owner],
            device_id=in_z(k),
            device_id_type=MESH,
        )

    @pl.loop(1, nz)
    def _(d):
        k = (zi + d) % nz

        @pl.when(k < owners)
        def _():
            z_copy(k, zi).start()

    @pl.when(zi < owners)
    def _():
        mine = rows_of(zi, zrows)
        ztot[mine, :] = zacc[mine, :]

        @pl.loop(1, nz)
        def _(d):
            k = (zi + d) % nz
            z_copy(zi, k).wait_recv()
            ztot[mine, :] += zrecv[k]

        @pl.loop(1, nz)
        def _(d):
            z_back(zi, (zi + d) % nz).start()

    @pl.loop(1, nz)
    def _(d):
        k = (zi + d) % nz

        @pl.when(k < owners)
        def _():
            z_copy(k, zi).wait_send()
            z_back(k, k).wait_recv()

    def plane_back(owner, k):
        return pltpu.make_async_remote_copy(
            src_ref=abuf.at[rows_of(owner, chunk)],
            dst_ref=abuf.at[rows_of(owner, chunk)],
            send_sem=xas.at[k],
            recv_sem=xar.at[owner],
            device_id=in_plane(k),
            device_id_type=MESH,
        )

    abuf[rows_of(plane, chunk), :] = ztot[...].astype(BF16)

    @pl.loop(1, nplane)
    def _(d):
        plane_back(plane, (plane + d) % nplane).start()

    @pl.when(zi < owners)
    def _():
        @pl.loop(1, nz)
        def _(d):
            z_back(zi, (zi + d) % nz).wait_send()

    @pl.loop(1, nplane)
    def _(d):
        k = (plane + d) % nplane
        plane_back(k, k).wait()

    last = pltpu.make_async_remote_copy(
        src_ref=abuf,
        dst_ref=fin,
        send_sem=core_s.at[2],
        recv_sem=core_r.at[2],
        device_id=pair,
        device_id_type=MESH,
    )
    last.start()
    total[core] = abuf[...]
    last.wait()
    total[1 - core] = fin[...]


def finish_kernel(factor, total, block, grad, block_out, grad_out, gk, gg, gb, gw_in, gbh, gw_out, gbo, gls):
    block_out[...] = block[...]
    grad_out[...] = grad[...]
    for t in range(HID // 128):
        rows = slice(t * C, (t + 1) * C)
        wide = slice(128 * t, 128 * t + 128)
        gw_in[:, wide] = total[0, rows, :].astype(F32) * factor
        gw_out[:, wide] = total[1, rows, :].astype(F32) * factor
    hi, lo = slice(WROWS, WROWS + SROWS), slice(WROWS + SROWS, TOT)
    left = (total[0, hi, :].astype(F32) + total[0, lo, :].astype(F32)) * factor
    right = (total[1, hi, :].astype(F32) + total[1, lo, :].astype(F32)) * factor
    for a in range(7):
        gk[a, :, 0:128] = left[7 * a : 7 * a + 7]
        gk[a, :, 128:C] = right[7 * a : 7 * a + 7, 0 : C - 128]
    for i, out in enumerate((gg, gb, gbo, gls)):
        out[:, 0:128] = left[49 + i : 50 + i]
        out[:, 128:C] = right[49 + i : 50 + i, 0 : C - 128]
    for i in range(3):
        gbh[:, 256 * i : 256 * i + 128] = left[53 + i : 54 + i]
        gbh[:, 256 * i + 128 : 256 * i + 256] = right[53 + i : 54 + i]


def on_device(
    nlon,
    nlat,
    state,
    land_mask,
    cotangent,
    kernel,
    norm_gain,
    norm_bias,
    weight_in,
    bias_hidden,
    weight_out,
    bias_out,
    layer_scale,
):
    px, nzl, nzh, py = groups(nlon, nlat)
    nplane, nz = px * py, nzl * nzh
    chunk = TOT // nplane
    zrows = max(8, -(-chunk // nz // 8) * 8)
    if zrows * nz < chunk:
        zrows += 8
    vmem = pl.BlockSpec(memory_space=pltpu.VMEM)
    dma = pltpu.SemaphoreType.DMA
    row = lambda v: v.reshape(1, -1)
    block, grad, total = pl.pallas_call(
        functools.partial(main_kernel, nlon, nlat),
        out_shape=(
            jax.ShapeDtypeStruct((ROWS, COLS, C), BF16),
            jax.ShapeDtypeStruct((ROWS, COLS, C), BF16),
            jax.ShapeDtypeStruct((2, TOT, 128), BF16),
        ),
        in_specs=[vmem] * 11,
        out_specs=(vmem,) * 3,
        scratch_shapes=[
            pltpu.VMEM((PADR, WIDE, C), F32),
            pltpu.VMEM((7, PADR, 2, 8, C), F32),
            pltpu.VMEM((PADR, WIDE, C), F32),
            pltpu.VMEM((7, PADR, 2, 8, C), F32),
            pltpu.VMEM((49, 8, C), F32),
            pltpu.VMEM((ROWS, COLS, C), F32),
            pltpu.VMEM((CELLS, C), BF16),
            pltpu.VMEM((CELLS, HID), BF16),
            pltpu.VMEM((CELLS, HID), BF16),
            pltpu.VMEM((CELLS, C), BF16),
            pltpu.VMEM((CELLS, C), BF16),
            pltpu.VMEM((4, 8, C), F32),
            pltpu.VMEM((8, HID), F32),
            pltpu.VMEM((SROWS, 256), F32),
            pltpu.VMEM((2, 2, 96, C), BF16),
            pltpu.VMEM((2, 2, 96, C), BF16),
            pltpu.VMEM((2, 2, 3, WIDE, C), BF16),
            pltpu.VMEM((2, 2, 3, WIDE, C), BF16),
            pltpu.VMEM((2, WROWS + SROWS, 128), F32),
            pltpu.VMEM((WROWS + SROWS, 128), F32),
            pltpu.VMEM((TOT, 128), F32),
            pltpu.VMEM((TOT, 128), BF16),
            pltpu.VMEM((nplane, chunk, 128), BF16),
            pltpu.VMEM((chunk, 128), F32),
            pltpu.VMEM((nz, zrows, 128), F32),
            pltpu.VMEM((chunk, 128), F32),
            pltpu.VMEM((TOT, 128), BF16),
            pltpu.VMEM((TOT, 128), BF16),
            dma((2, 2)),
            dma((2, 2)),
            dma((2, 2)),
            dma((2, 2)),
            dma((3,)),
            dma((3,)),
            dma((nplane,)),
            dma((nplane,)),
            dma((nz,)),
            dma((nz,)),
            dma((nz,)),
            dma((nz,)),
            dma((nplane,)),
            dma((nplane,)),
        ],
        compiler_params=pltpu.CompilerParams(
            collective_id=0, has_side_effects=True, vmem_limit_bytes=48 * 1024 * 1024
        ),
        name="block",
    )(
        state,
        land_mask.T,
        cotangent,
        kernel,
        row(norm_gain),
        row(norm_bias),
        weight_in,
        row(bias_hidden),
        weight_out.T,
        row(bias_out),
        row(layer_scale),
    )
    factor = 1.0 / math.sqrt(ROWS * nlat * COLS * nlon)
    shape = lambda *s: jax.ShapeDtypeStruct(s, F32)
    outs = pl.pallas_call(
        functools.partial(finish_kernel, factor),
        out_shape=(
            jax.ShapeDtypeStruct((ROWS, COLS, C), BF16),
            jax.ShapeDtypeStruct((ROWS, COLS, C), BF16),
            shape(7, 7, C),
            shape(1, C),
            shape(1, C),
            shape(C, HID),
            shape(1, HID),
            shape(C, HID),
            shape(1, C),
            shape(1, C),
        ),
        in_specs=[vmem] * 3,
        out_specs=(vmem,) * 10,
        compiler_params=pltpu.CompilerParams(vmem_limit_bytes=32 * 1024 * 1024),
        name="finish",
    )(total, block, grad)
    outs = [o.reshape(-1) if o.shape[0] == 1 else o for o in outs]
    outs[7] = outs[7].T
    return tuple(outs)


def solution(mesh):
    cells, plane, whole = P("lat", "lon", None), P("lat", "lon"), P()
    return jax.shard_map(
        functools.partial(on_device, mesh.shape["lon"], mesh.shape["lat"]),
        mesh=mesh,
        in_specs=(cells, plane, cells) + (whole,) * 8,
        out_specs=(cells, cells) + (whole,) * 8,
        check_vma=False,
    )
```

```python
import functools
import math

import jax
import jax.numpy as jnp
from jax import lax
from jax.experimental import pallas as pl
from jax.experimental.pallas import tpu as pltpu
from jax.sharding import PartitionSpec as P

EPSILON = 1e-06
MESH = pl.DeviceIdType.MESH
F32 = jnp.float32
BF16 = jnp.bfloat16

ROWS, COLS, C, HID = 32, 16, 192, 768
CELLS = ROWS * COLS
PADR, WIDE = ROWS + 6, 32
WROWS = C * HID // 128
SROWS = 64
TOT = WROWS + 2 * SROWS
MAIN = 1024
GELU_A = math.sqrt(2.0 / math.pi)
GELU_B = 0.044715


def groups(nlon, nlat):
    px = 4 if nlon >= 64 else 1
    nzl = nlon // (2 * px)
    nzh = 2 if nlat >= 8 else 1
    return px, nzl, nzh, nlat // nzh


def shares(nlon, nlat):
    px, nzl, nzh, py = groups(nlon, nlat)
    size = px * py * 2
    return size, nzl * nzh // 2, MAIN // size, max(16, (TOT - MAIN) // size)


def one_hot(shape, pick):
    a = lax.broadcasted_iota(jnp.int32, shape, 0)
    b = lax.broadcasted_iota(jnp.int32, shape, 1)
    return pick(a, b).astype(F32).astype(BF16)


def dot(a, b, contract=((1,), (0,))):
    return lax.dot_general(a, b, (contract, ((), ())), preferred_element_type=F32)


def remote(kind, src, dst, send, recv, target):
    return pltpu.make_async_remote_copy(
        src_ref=src,
        dst_ref=dst,
        send_sem=send,
        recv_sem=recv,
        device_id=target,
        device_id_type=MESH,
    )


def main_kernel(
    nlon,
    nlat,
    state_h,
    mask_h,
    cot_h,
    kern_h,
    gain_h,
    nbias_h,
    w_in_h,
    b_hid_h,
    w_out_h,
    b_out_h,
    scale_h,
    block_h,
    grad_h,
    total,
    block_out,
    grad_state,
    state,
    mask,
    cot,
    kern,
    gain,
    nbias,
    w_in,
    b_hid,
    w_out,
    b_out,
    scale,
    pad,
    shifted,
    padq,
    shiftq,
    taps,
    maskb,
    normed_s,
    precot_s,
    hidden_s,
    bcot_s,
    own_s,
    sums,
    sumh,
    small,
    csend,
    ksend,
    crecv,
    vrecv,
    wbuf,
    wrecv,
    psum,
    extra,
    pay,
    xrecv,
    zslot,
    abuf,
    fin,
    load_s,
    store_s,
    halo_s,
    halo_r,
    core_s,
    core_r,
    xs,
    xr,
    zs,
    zr,
    xas,
    xar,
):
    px, nzl, nzh, py = groups(nlon, nlat)
    size, nz, mrows, erows = shares(nlon, nlat)

    loads = [
        pltpu.make_async_copy(src, dst, load_s.at[i])
        for i, (src, dst) in enumerate(
            (
                (state_h, state),
                (mask_h, mask),
                (kern_h, kern),
                (cot_h, cot),
                (w_in_h, w_in),
                (w_out_h, w_out),
                (gain_h, gain),
                (nbias_h, nbias),
                (b_hid_h, b_hid),
                (b_out_h, b_out),
                (scale_h, scale),
            )
        )
    ]
    for load in loads[:3]:
        load.start()

    lon = lax.axis_index("lon")
    lat = lax.axis_index("lat")
    core = lax.rem(lon, 2)
    x = lax.rem(lax.div(lon, 2), px)
    zl = lax.div(lon, 2 * px)
    zh = lax.rem(lat, nzh)
    y = lax.div(lat, nzh)
    odd = lax.rem(zl, 2)
    me = (y * px + x) * 2 + odd
    zi = zh * (nzl // 2) + lax.div(zl, 2)
    is_top = lat == nlat - 1
    has_south = lat > 0

    def device(la, lo):
        return {"lon": lo, "lat": la}

    right, left = lax.rem(lon + 1, nlon), lax.rem(lon + nlon - 1, nlon)
    above, below = jnp.where(is_top, lat, lat + 1), jnp.where(has_south, lat - 1, 0)
    fold_r, fold_l = lax.rem(2 * nlon - 2 - lon, nlon), lax.rem(nlon - lon, nlon)
    east, west = device(lat, right), device(lat, left)
    north = device(above, jnp.where(is_top, nlon - 1 - lon, lon))
    south = device(below, lon)
    top_r = device(above, jnp.where(is_top, fold_r, right))
    top_l = device(above, jnp.where(is_top, fold_l, left))
    bot_r, bot_l = device(below, right), device(below, left)
    self_r = jnp.logical_and(is_top, fold_r == lon)
    self_l = jnp.logical_and(is_top, fold_l == lon)
    other_r, other_l = jnp.logical_not(self_r), jnp.logical_not(self_l)
    pair = device(lat, lon + 1 - 2 * core)

    def in_group(k):
        p = lax.div(k, 2)
        z = zl - odd + lax.rem(k, 2)
        return device(lax.div(p, px) * nzh + zh, z * (2 * px) + lax.rem(p, px) * 2 + core)

    def in_z(k):
        z = lax.rem(k, nzl // 2) * 2 + odd
        return device(y * nzh + lax.div(k, nzl // 2), z * (2 * px) + x * 2 + core)

    def shift(field, out):
        @pl.loop(0, PADR)
        def _(r):
            for b in range(7):
                out[b, r] = field[r, 5 + b : 21 + b, :].reshape(2, 8, C)

    def conv_rows(source, r0, rows, flip):
        acc = jnp.zeros((rows, 2, 8, C), F32)
        for b in range(7):
            for a in range(7):
                k = taps[48 - a * 7 - b] if flip else taps[a * 7 + b]
                acc = acc + source[b, pl.ds(r0 + a, rows)] * k
        return acc

    barrier = pltpu.get_barrier_semaphore()

    def hello(target):
        pl.semaphore_signal(barrier, inc=1, device_id=target, device_id_type=MESH)

    hello(north)

    @pl.when(has_south)
    def _():
        hello(south)
        hello(bot_r)
        hello(bot_l)

    @pl.when(other_r)
    def _():
        hello(top_r)

    @pl.when(other_l)
    def _():
        hello(top_l)

    hello(east)
    hello(west)

    @pl.loop(1, nz)
    def _(d):
        hello(in_z(lax.rem(zi + d, nz)))

    @pl.loop(1, size)
    def _(d):
        hello(in_group(lax.rem(me + d, size)))

    hello(pair)
    for load in loads[3:]:
        load.start()

    by_row = one_hot((CELLS, ROWS), lambda a, b: a // COLS == b)
    by_col = one_hot((CELLS, COLS), lambda a, b: a % COLS == b).astype(F32)

    def pick_cell(a):
        e = (a // 3) * COLS + 13 + a % 3
        w = ((a - 96) // 3) * COLS + (a - 96) % 3
        c, i = (a - 192) // 16, (a - 192) % 16
        corner = (i // 3 + (ROWS - 3) * (c // 2)) * COLS + i % 3 + 13 * (c % 2)
        return jnp.where(a < 96, e, jnp.where(a < 192, w, jnp.where(i < 9, corner, -1)))

    picks = one_hot((256, CELLS), lambda a, b: pick_cell(a) == b)
    left_put = one_hot(
        (ROWS * 8, 96), lambda a, b: (a % 8 >= 5) & ((a // 8) * 3 + a % 8 - 5 == b)
    )
    right_put = one_hot((ROWS * 8, 96), lambda a, b: (a % 8 < 3) & ((a // 8) * 3 + a % 8 == b))

    def put_cell(a, fold):
        m, q = a // WIDE, a % WIDE
        row = jnp.where(fold, 2 - m, m)
        mid = row * COLS + jnp.where(fold, 23 - q, q - 8)
        lo = 48 + row * 3 + jnp.where(fold, 7 - q, q - 5)
        hi = 64 + row * 3 + jnp.where(fold, 26 - q, q - 24)
        hi = jnp.where((q >= 24) & (q < 27), hi, -1)
        return jnp.where((q >= 8) & (q < 24), mid, jnp.where((q >= 5) & (q < 8), lo, hi))

    north_put = one_hot((3 * WIDE, 80), lambda a, b: put_cell(a, is_top) == b)
    south_put = one_hot((3 * WIDE, 80), lambda a, b: put_cell(a, False) == b)

    def halo_copies(n):
        slot = jnp.where(is_top, 0, 1)

        def copy(src, dst, s, r, target):
            return remote("halo", src, dst, halo_s.at[n, s], halo_r.at[n, r], target)

        corner = ksend.at[n]
        return dict(
            e=copy(csend.at[n, 0], crecv.at[n, 0], 0, 0, east),
            w=copy(csend.at[n, 1], crecv.at[n, 1], 1, 1, west),
            up=copy(own_s.at[n, ROWS - 3 : ROWS], vrecv.at[n, slot, 0:3], 2, 2 + slot, north),
            tr=copy(
                corner.at[3],
                vrecv.at[n, slot, 4 - slot],
                3,
                jnp.where(is_top, 5, 6),
                top_r,
            ),
            tl=copy(
                corner.at[2],
                vrecv.at[n, slot, 3 + slot],
                4,
                jnp.where(is_top, 4, 7),
                top_l,
            ),
            down=copy(own_s.at[n, 0:3], vrecv.at[n, 0, 0:3], 5, 2, south),
            br=copy(corner.at[1], vrecv.at[n, 0, 3], 6, 4, bot_r),
            bl=copy(corner.at[0], vrecv.at[n, 0, 4], 7, 5, bot_l),
        )

    def pick_halo(n):
        picked = dot(picks, own_s[n].reshape(CELLS, C)).astype(BF16)
        csend[n] = picked[0:192].reshape(2, 96, C)
        ksend[n] = picked[192:256].reshape(4, 16, C)

    def send_halo(n):
        copies = halo_copies(n)
        copies["up"].start()

        @pl.when(has_south)
        def _():
            copies["down"].start()
            copies["br"].start()
            copies["bl"].start()

        @pl.when(other_r)
        def _():
            copies["tr"].start()

        @pl.when(other_l)
        def _():
            copies["tl"].start()

        copies["e"].start()
        copies["w"].start()

        @pl.when(self_r)
        def _():
            vrecv[n, 0, 4] = ksend[n, 3]

        @pl.when(self_l)
        def _():
            vrecv[n, 0, 3] = ksend[n, 2]

    def take_halo(n, field):
        copies = halo_copies(n)

        def arrive(piece, r):
            remote("halo", piece, piece, halo_s.at[n, 0], halo_r.at[n, r], east).wait_recv()

        copies["e"].wait()
        copies["w"].wait()
        field[3 : 3 + ROWS, 0:8, :] = dot(left_put, crecv[n, 0]).reshape(ROWS, 8, C)
        field[3 : 3 + ROWS, 24:32, :] = dot(right_put, crecv[n, 1]).reshape(ROWS, 8, C)
        copies["up"].wait_send()
        arrive(vrecv.at[n, 0, 0:3], 2)

        @pl.when(other_r)
        def _():
            copies["tr"].wait_send()
            arrive(vrecv.at[n, 0, 4], 5)

        @pl.when(other_l)
        def _():
            copies["tl"].wait_send()
            arrive(vrecv.at[n, 0, 3], 4)

        field[ROWS + 3 : ROWS + 6] = dot(north_put, vrecv[n, 0].reshape(80, C)).reshape(3, WIDE, C)

        @pl.when(has_south)
        def _():
            for name in ("down", "br", "bl"):
                copies[name].wait_send()
            arrive(vrecv.at[n, 1, 0:3], 3)
            arrive(vrecv.at[n, 1, 3], 6)
            arrive(vrecv.at[n, 1, 4], 7)
            field[0:3] = dot(south_put, vrecv[n, 1].reshape(80, C)).reshape(3, WIDE, C)

        @pl.when(jnp.logical_not(has_south))
        def _():
            field[0:3] = jnp.zeros((3, WIDE, C), F32)

    for load in loads[:3]:
        load.wait()
    sea = dot(by_row, mask[...].astype(F32).astype(BF16), ((1,), (1,))) * by_col
    maskb[...] = dot(sea.astype(BF16), jnp.ones((COLS, C), BF16)).reshape(ROWS, COLS, C)
    own = state[...].astype(F32) * maskb[...]
    pad[3 : 3 + ROWS, 8:24, :] = own
    own_s[0] = own.astype(BF16)
    pick_halo(0)
    for a in range(7):
        k7 = kern[a].astype(F32)
        for b in range(7):
            taps[a * 7 + b] = jnp.broadcast_to(k7[b : b + 1], (8, C))
    sums[...] = jnp.zeros_like(sums)
    sumh[...] = jnp.zeros_like(sumh)
    small[...] = jnp.zeros_like(small)
    extra[...] = jnp.zeros_like(extra)

    hellos = 4 + (size - 1) + (nz - 1) + jnp.where(has_south, 3, 0)
    hellos = hellos + jnp.where(other_r, 1, 0) + jnp.where(other_l, 1, 0)
    pl.semaphore_wait(barrier, hellos)
    send_halo(0)
    for load in loads[3:]:
        load.wait()
    take_halo(0, pad)
    shift(pad, shifted)

    block = 8
    cells = block * COLS

    @pl.loop(0, ROWS // block)
    def _(blk):
        r0 = blk * block
        here = pl.ds(pl.multiple_of(r0 * COLS, cells), cells)
        mixed = jnp.concatenate(
            [conv_rows(shifted, r0 + 4 * i, 4, False).reshape(4 * COLS, C) for i in range(block // 4)],
            axis=0,
        )
        average = jnp.sum(mixed, axis=1, keepdims=True) * (1.0 / C)
        centred = mixed - average
        variance = jnp.sum(centred * centred, axis=1, keepdims=True) * (1.0 / C)
        inv_std = lax.rsqrt(variance + EPSILON)
        unit = centred * inv_std
        normed = (unit * gain[...] + nbias[...]).astype(BF16)
        normed_s[here, :] = normed
        pre = dot(normed, w_in[...]) + b_hid[...].reshape(HID)
        square = pre * pre
        t = jnp.tanh(GELU_A * pre * (1.0 + GELU_B * square))
        half = 0.5 * (1.0 + t)
        hidden = (pre * half).astype(BF16)
        hidden_s[here, :] = hidden
        slope = half + pre * (0.5 * GELU_A) * (1.0 - t * t) * (1.0 + 3.0 * GELU_B * square)
        branch = dot(hidden, w_out[...], ((1,), (1,))) + b_out[...]
        rows_here = pl.ds(r0, block)
        sea_w = maskb[rows_here].reshape(cells, C)
        st = state[rows_here].astype(F32).reshape(cells, C)
        ct = cot[rows_here].astype(F32).reshape(cells, C) * sea_w
        block_out[rows_here] = (
            (sea_w * (st + scale[...] * branch)).astype(BF16).reshape(block, COLS, C)
        )
        grad_branch = ct * scale[...]
        bcot = grad_branch.astype(BF16)
        bcot_s[here, :] = bcot
        grad_pre = dot(bcot, w_out[...]) * slope
        precot = grad_pre.astype(BF16)
        precot_s[here, :] = precot
        grad_normed = dot(precot, w_in[...], ((1,), (1,)))
        grad_unit = grad_normed * gain[...]
        mean_a = jnp.sum(grad_unit, axis=1, keepdims=True) * (1.0 / C)
        mean_b = jnp.sum(grad_unit * unit, axis=1, keepdims=True) * (1.0 / C)
        grad_mixed = inv_std * (grad_unit - mean_a - unit * mean_b)
        mcot = grad_mixed.astype(BF16)
        own_s[1, rows_here] = mcot.reshape(block, COLS, C)
        padq[pl.ds(3 + r0, block), 8:24, :] = mcot.astype(F32).reshape(block, COLS, C)

        def fold8(v):
            return jnp.sum(v.reshape(cells // 8, 8, v.shape[1]), axis=0)

        sums[0] += fold8(grad_normed * unit)
        sums[1] += fold8(grad_normed)
        sums[2] += fold8(grad_branch)
        sums[3] += fold8(ct * branch)
        sumh[...] += fold8(grad_pre)

    pick_halo(1)
    send_halo(1)
    block_store = pltpu.make_async_copy(block_out, block_h, store_s.at[0])
    block_store.start()

    for t in range(HID // 256):
        wide = slice(256 * t, 256 * t + 256)
        g_in = dot(normed_s[...], precot_s[:, wide], ((0,), (0,)))
        g_out = dot(bcot_s[...], hidden_s[:, wide], ((0,), (0,)))
        for j in range(2):
            to = slice((2 * t + j) * C, (2 * t + j + 1) * C)
            wbuf[0, to, :] = g_in[:, 128 * j : 128 * j + 128]
            wbuf[1, to, :] = g_out[:, 128 * j : 128 * j + 128]

    def to_pair(i, rows):
        return remote("pair", wbuf.at[1 - core, rows], wrecv.at[rows], core_s.at[i], core_r.at[i], pair)

    pair_w = to_pair(0, pl.ds(0, WROWS))
    pair_w.start()

    for b in range(7):

        def step(i, accs, b=b):
            r0 = i * 4
            m = padq[pl.ds(3 + r0, 4), 8:24, :].reshape(4, 2, 8, C)
            return tuple(
                accs[a] + jnp.sum((m * shifted[b, pl.ds(r0 + a, 4)]).reshape(8, 8, C), axis=0)
                for a in range(7)
            )

        accs = lax.fori_loop(0, ROWS // 4, step, tuple(jnp.zeros((8, C), F32) for _ in range(7)))
        for a in range(7):
            small[a * 7 + b : a * 7 + b + 1, 0:C] = jnp.sum(accs[a], axis=0, keepdims=True)
    for i in range(4):
        small[49 + i : 50 + i, 0:C] = jnp.sum(sums[i], axis=0, keepdims=True)
    hid_row = jnp.sum(sumh[...], axis=0, keepdims=True)
    for i in range(3):
        small[53 + i : 54 + i, :] = hid_row[:, 256 * i : 256 * i + 256]
    wbuf[0, WROWS:, :] = small[:, 0:128]
    wbuf[1, WROWS:, :] = small[:, 128:256]
    pair_s = to_pair(1, pl.ds(WROWS, SROWS))
    pair_s.start()

    pair_w.wait()

    @pl.loop(0, size)
    def _(k):
        rows = pl.ds(pl.multiple_of(k * mrows, 32), mrows)
        both = wbuf[core, rows, :] + wrecv[rows, :]
        psum[rows, :] = both
        pay[k, 0:mrows, :] = both.astype(BF16)

    pair_s.wait()
    rest_w = wbuf[core, MAIN:WROWS, :] + wrecv[MAIN:WROWS, :]
    both = wbuf[core, WROWS:, :] + wrecv[WROWS:, :]
    high = both.astype(BF16).astype(F32)
    other = jnp.concatenate([rest_w, high, both - high], axis=0)
    for i in range((TOT - MAIN) // size):
        extra[pl.ds(i, size, stride=erows), :] = other[i * size : (i + 1) * size]
    pay[:, mrows:, :] = extra[...].reshape(size, erows, 128).astype(BF16)

    def group_copy(k, sender):
        return remote("group", pay.at[k], xrecv.at[sender], xs.at[k], xr.at[sender], in_group(k))

    @pl.loop(1, size)
    def _(d):
        k = lax.rem(me + d, size)
        group_copy(k, me).start()

    def halves(v):
        first = (WROWS - MAIN) // size
        count = SROWS // size
        end = v.shape[0]
        row = lax.broadcasted_iota(jnp.int32, v.shape, 0) - mrows
        whole = v + pltpu.roll(v, end - count, 0)
        top = whole.astype(BF16).astype(F32)
        low = pltpu.roll(whole - top, count, 0)
        is_high = (row >= first) & (row < first + count)
        is_low = (row >= first + count) & (row < first + 2 * count)
        return jnp.where(is_high, top, jnp.where(is_low, low, v)).astype(BF16)

    @pl.loop(1, size)
    def _(d):
        k = lax.rem(me + d, size)
        group_copy(k, k).wait()

    def add_chunk(d, acc):
        return acc + xrecv[lax.rem(me + d, size)].astype(F32)

    mine = jnp.concatenate(
        [
            psum[pl.ds(pl.multiple_of(me * mrows, 32), mrows), :],
            extra[pl.ds(pl.multiple_of(me * erows, 16), erows), :],
        ],
        axis=0,
    )
    zslot[zi] = halves(lax.fori_loop(1, size, add_chunk, mine))

    def z_copy(k, sender):
        return remote("z", zslot.at[sender], zslot.at[sender], zs.at[k], zr.at[sender], in_z(k))

    @pl.loop(1, nz)
    def _(d):
        z_copy(lax.rem(zi + d, nz), zi).start()

    take_halo(1, padq)
    shift(padq, shiftq)

    @pl.loop(0, ROWS // 4)
    def _(i):
        rows_here = pl.ds(i * 4, 4)
        grad = conv_rows(shiftq, i * 4, 4, True).reshape(4, COLS, C)
        grad_state[rows_here] = (
            maskb[rows_here] * (cot[rows_here].astype(F32) + grad)
        ).astype(BF16)

    @pl.when(is_top)
    def _():
        first = ROWS - 4
        acc = conv_rows(shiftq, first, 4, True)
        parts = [acc[i] for i in range(4)]
        for i in range(1, 4):
            for a in range(7 - i, 7):
                for b in range(7):
                    change = taps[a * 7 + b] - taps[48 - a * 7 - b]
                    parts[i] = parts[i] + shiftq[b, first + i + a] * change
        for i in range(1, 4):
            grad_state[first + i] = (
                maskb[first + i] * (cot[first + i].astype(F32) + parts[i].reshape(COLS, C))
            ).astype(BF16)

    grad_store = pltpu.make_async_copy(grad_state, grad_h, store_s.at[1])
    grad_store.start()

    @pl.loop(1, nz)
    def _(d):
        k = lax.rem(zi + d, nz)
        z_copy(k, k).wait()

    whole = zslot[0].astype(F32)
    for k in range(1, nz):
        whole = whole + zslot[k].astype(F32)
    abuf[me] = halves(whole)

    def back_copy(owner, k):
        return remote("back", abuf.at[owner], abuf.at[owner], xas.at[k], xar.at[owner], in_group(k))

    @pl.loop(1, size)
    def _(d):
        back_copy(me, lax.rem(me + d, size)).start()

    @pl.loop(1, size)
    def _(d):
        k = lax.rem(me + d, size)
        back_copy(k, k).wait()

    last = remote("last", abuf, fin, core_s.at[2], core_r.at[2], pair)
    last.start()
    own_store = pltpu.make_async_copy(abuf, total.at[core], store_s.at[2])
    own_store.start()
    last.wait()
    fin_store = pltpu.make_async_copy(fin, total.at[1 - core], store_s.at[3])
    fin_store.start()
    for store in (block_store, grad_store, own_store, fin_store):
        store.wait()


def finish_kernel(
    factor, size, mrows, erows, total_h, block, grad,
    block_out, grad_out, gk, gg, gb, gw_in, gbh, gw_out, gbo, gls, total, extra, sem,
):
    moves = [
        pltpu.make_async_copy(src, dst, sem.at[i])
        for i, (src, dst) in enumerate(
            ((total_h, total), (block, block_out), (grad, grad_out))
        )
    ]
    for move in moves:
        move.start()
    moves[0].wait()
    small = []
    for c, gw in ((0, gw_in), (1, gw_out)):
        rows = total[c, :, 0:mrows, :].reshape(MAIN, 128).astype(F32) * factor
        extra[...] = total[c, :, mrows:, :].reshape(size * erows, 128).astype(F32) * factor
        rest = [extra[pl.ds(i, size, stride=erows), :] for i in range((TOT - MAIN) // size)]
        rows = jnp.concatenate([rows] + rest, axis=0)
        for t in range(HID // 128):
            gw[:, 128 * t : 128 * t + 128] = rows[t * C : (t + 1) * C]
        small.append(rows[WROWS : WROWS + SROWS] + rows[WROWS + SROWS :])
    near, far = small
    for a in range(7):
        gk[a, :, 0:128] = near[7 * a : 7 * a + 7]
        gk[a, :, 128:C] = far[7 * a : 7 * a + 7, 0 : C - 128]
    for i, out in enumerate((gg, gb, gbo, gls)):
        out[:, 0:128] = near[49 + i : 50 + i]
        out[:, 128:C] = far[49 + i : 50 + i, 0 : C - 128]
    for i in range(3):
        gbh[256 * i : 256 * i + 128] = near[53 + i]
        gbh[256 * i + 128 : 256 * i + 256] = far[53 + i]
    for move in moves[1:]:
        move.wait()


def on_device(
    nlon,
    nlat,
    state,
    land_mask,
    cotangent,
    kernel,
    norm_gain,
    norm_bias,
    weight_in,
    bias_hidden,
    weight_out,
    bias_out,
    layer_scale,
):
    size, nz, mrows, erows = shares(nlon, nlat)
    hbm = pl.BlockSpec(memory_space=pltpu.HBM)
    vmem = pl.BlockSpec(memory_space=pltpu.VMEM)
    dma = pltpu.SemaphoreType.DMA
    row = lambda v: v.reshape(1, -1)
    block, grad, total = pl.pallas_call(
        functools.partial(main_kernel, nlon, nlat),
        out_shape=(
            jax.ShapeDtypeStruct((ROWS, COLS, C), BF16),
            jax.ShapeDtypeStruct((ROWS, COLS, C), BF16),
            jax.ShapeDtypeStruct((2, size, mrows + erows, 128), BF16),
        ),
        in_specs=[hbm] * 11,
        out_specs=(hbm,) * 3,
        scratch_shapes=[
            pltpu.VMEM((ROWS, COLS, C), BF16),
            pltpu.VMEM((ROWS, COLS, C), BF16),
            pltpu.VMEM((ROWS, COLS, C), BF16),
            pltpu.VMEM((COLS, ROWS), jnp.int32),
            pltpu.VMEM((ROWS, COLS, C), BF16),
            pltpu.VMEM((7, 7, C), BF16),
            pltpu.VMEM((1, C), F32),
            pltpu.VMEM((1, C), F32),
            pltpu.VMEM((C, HID), BF16),
            pltpu.VMEM((HID,), F32),
            pltpu.VMEM((C, HID), BF16),
            pltpu.VMEM((1, C), F32),
            pltpu.VMEM((1, C), F32),
            pltpu.VMEM((PADR, WIDE, C), F32),
            pltpu.VMEM((7, PADR, 2, 8, C), F32),
            pltpu.VMEM((PADR, WIDE, C), F32),
            pltpu.VMEM((7, PADR, 2, 8, C), F32),
            pltpu.VMEM((49, 8, C), F32),
            pltpu.VMEM((ROWS, COLS, C), F32),
            pltpu.VMEM((CELLS, C), BF16),
            pltpu.VMEM((CELLS, HID), BF16),
            pltpu.VMEM((CELLS, HID), BF16),
            pltpu.VMEM((CELLS, C), BF16),
            pltpu.VMEM((2, ROWS, COLS, C), BF16),
            pltpu.VMEM((4, 8, C), F32),
            pltpu.VMEM((8, HID), F32),
            pltpu.VMEM((SROWS, 256), F32),
            pltpu.VMEM((2, 2, 96, C), BF16),
            pltpu.VMEM((2, 4, 16, C), BF16),
            pltpu.VMEM((2, 2, 96, C), BF16),
            pltpu.VMEM((2, 2, 5, 16, C), BF16),
            pltpu.VMEM((2, WROWS + SROWS, 128), F32),
            pltpu.VMEM((WROWS + SROWS, 128), F32),
            pltpu.VMEM((MAIN, 128), F32),
            pltpu.VMEM((size * erows, 128), F32),
            pltpu.VMEM((size, mrows + erows, 128), BF16),
            pltpu.VMEM((size, mrows + erows, 128), BF16),
            pltpu.VMEM((nz, mrows + erows, 128), BF16),
            pltpu.VMEM((size, mrows + erows, 128), BF16),
            pltpu.VMEM((size, mrows + erows, 128), BF16),
            dma((11,)),
            dma((4,)),
            dma((2, 8)),
            dma((2, 8)),
            dma((3,)),
            dma((3,)),
            dma((size,)),
            dma((size,)),
            dma((nz,)),
            dma((nz,)),
            dma((size,)),
            dma((size,)),
        ],
        compiler_params=pltpu.CompilerParams(
            collective_id=0, has_side_effects=True, vmem_limit_bytes=56 * 1024 * 1024
        ),
        name="block",
    )(
        state,
        land_mask.T,
        cotangent,
        kernel,
        row(norm_gain),
        row(norm_bias),
        weight_in,
        bias_hidden,
        weight_out.T,
        row(bias_out),
        row(layer_scale),
    )
    factor = 1.0 / math.sqrt(ROWS * nlat * COLS * nlon)
    shape = lambda *s: jax.ShapeDtypeStruct(s, F32)
    outs = pl.pallas_call(
        functools.partial(finish_kernel, factor, size, mrows, erows),
        out_shape=(
            jax.ShapeDtypeStruct((ROWS, COLS, C), BF16),
            jax.ShapeDtypeStruct((ROWS, COLS, C), BF16),
            shape(7, 7, C),
            shape(1, C),
            shape(1, C),
            shape(C, HID),
            shape(HID),
            shape(C, HID),
            shape(1, C),
            shape(1, C),
        ),
        in_specs=[hbm] * 3,
        out_specs=(hbm,) * 2 + (vmem,) * 8,
        scratch_shapes=[
            pltpu.VMEM((2, size, mrows + erows, 128), BF16),
            pltpu.VMEM((size * erows, 128), F32),
            dma((3,)),
        ],
        compiler_params=pltpu.CompilerParams(vmem_limit_bytes=56 * 1024 * 1024),
        name="finish",
    )(total, block, grad)
    outs = [o.reshape(-1) if o.shape[0] == 1 else o for o in outs]
    outs[7] = outs[7].T
    return tuple(outs)


def solution(mesh):
    cells, plane, whole = P("lat", "lon", None), P("lat", "lon"), P()
    return jax.shard_map(
        functools.partial(on_device, mesh.shape["lon"], mesh.shape["lat"]),
        mesh=mesh,
        in_specs=(cells, plane, cells) + (whole,) * 8,
        out_specs=(cells, cells) + (whole,) * 8,
        check_vma=False,
    )
```

```python
import functools
import math

import jax
import jax.numpy as jnp
from jax import lax
from jax.experimental import pallas as pl
from jax.experimental.pallas import tpu as pltpu
from jax.sharding import PartitionSpec as P

EPSILON = 1e-06
MESH = pl.DeviceIdType.MESH
F32 = jnp.float32
BF16 = jnp.bfloat16

ROWS, COLS, C, HID = 32, 16, 192, 768
CELLS = ROWS * COLS
PADR, WIDE = ROWS + 6, 32
WROWS = C * HID // 128
SROWS = 64
TOT = WROWS + 2 * SROWS
MAIN = 1024
GELU_A = math.sqrt(2.0 / math.pi)
GELU_B = 0.044715


def groups(nlon, nlat):
    px = 4 if nlon >= 64 else 1
    nzl = nlon // (2 * px)
    nzh = 2 if nlat >= 8 else 1
    return px, nzl, nzh, nlat // nzh


def shares(nlon, nlat):
    px, nzl, nzh, py = groups(nlon, nlat)
    size = px * py * 2
    return size, nzl * nzh // 2, MAIN // size, max(16, (TOT - MAIN) // size)


def one_hot(shape, pick):
    a = lax.broadcasted_iota(jnp.int32, shape, 0)
    b = lax.broadcasted_iota(jnp.int32, shape, 1)
    return pick(a, b).astype(F32).astype(BF16)


def dot(a, b, contract=((1,), (0,))):
    return lax.dot_general(a, b, (contract, ((), ())), preferred_element_type=F32)


def remote(kind, src, dst, send, recv, target):
    return pltpu.make_async_remote_copy(
        src_ref=src,
        dst_ref=dst,
        send_sem=send,
        recv_sem=recv,
        device_id=target,
        device_id_type=MESH,
    )


def main_kernel(
    nlon,
    nlat,
    state_h,
    mask_h,
    cot_h,
    kern_h,
    gain_h,
    nbias_h,
    w_in_h,
    b_hid_h,
    w_out_h,
    b_out_h,
    scale_h,
    block_h,
    grad_h,
    total,
    block_out,
    grad_state,
    state,
    mask,
    cot,
    kern,
    gain,
    nbias,
    w_in,
    b_hid,
    w_out,
    b_out,
    scale,
    pad,
    shifted,
    padq,
    shiftq,
    taps,
    maskb,
    normed_s,
    precot_s,
    hidden_s,
    bcot_s,
    own_s,
    sums,
    sumh,
    small,
    csend,
    ksend,
    crecv,
    vrecv,
    wbuf,
    wrecv,
    psum,
    extra,
    pay,
    xrecv,
    zslot,
    abuf,
    fin,
    load_s,
    store_s,
    halo_s,
    halo_r,
    core_s,
    core_r,
    xs,
    xr,
    zs,
    zr,
    xas,
    xar,
):
    px, nzl, nzh, py = groups(nlon, nlat)
    size, nz, mrows, erows = shares(nlon, nlat)

    loads = [
        pltpu.make_async_copy(src, dst, load_s.at[i])
        for i, (src, dst) in enumerate(
            (
                (state_h, state),
                (mask_h, mask),
                (kern_h, kern),
                (cot_h, cot),
                (w_in_h, w_in),
                (w_out_h, w_out),
                (gain_h, gain),
                (nbias_h, nbias),
                (b_hid_h, b_hid),
                (b_out_h, b_out),
                (scale_h, scale),
            )
        )
    ]
    for load in loads[:3]:
        load.start()

    lon = lax.axis_index("lon")
    lat = lax.axis_index("lat")
    core = lax.rem(lon, 2)
    x = lax.rem(lax.div(lon, 2), px)
    zl = lax.div(lon, 2 * px)
    zh = lax.rem(lat, nzh)
    y = lax.div(lat, nzh)
    odd = lax.rem(zl, 2)
    me = (y * px + x) * 2 + odd
    zi = zh * (nzl // 2) + lax.div(zl, 2)
    is_top = lat == nlat - 1
    has_south = lat > 0

    def device(la, lo):
        return {"lon": lo, "lat": la}

    right, left = lax.rem(lon + 1, nlon), lax.rem(lon + nlon - 1, nlon)
    above, below = jnp.where(is_top, lat, lat + 1), jnp.where(has_south, lat - 1, 0)
    fold_r, fold_l = lax.rem(2 * nlon - 2 - lon, nlon), lax.rem(nlon - lon, nlon)
    east, west = device(lat, right), device(lat, left)
    north = device(above, jnp.where(is_top, nlon - 1 - lon, lon))
    south = device(below, lon)
    top_r = device(above, jnp.where(is_top, fold_r, right))
    top_l = device(above, jnp.where(is_top, fold_l, left))
    bot_r, bot_l = device(below, right), device(below, left)
    self_r = jnp.logical_and(is_top, fold_r == lon)
    self_l = jnp.logical_and(is_top, fold_l == lon)
    other_r, other_l = jnp.logical_not(self_r), jnp.logical_not(self_l)
    pair = device(lat, lon + 1 - 2 * core)

    def in_group(k):
        p = lax.div(k, 2)
        z = zl - odd + lax.rem(k, 2)
        return device(lax.div(p, px) * nzh + zh, z * (2 * px) + lax.rem(p, px) * 2 + core)

    def in_z(k):
        z = lax.rem(k, nzl // 2) * 2 + odd
        return device(y * nzh + lax.div(k, nzl // 2), z * (2 * px) + x * 2 + core)

    def shift(field, out):
        @pl.loop(0, PADR)
        def _(r):
            for b in range(7):
                out[b, r] = field[r, 5 + b : 21 + b, :].reshape(2, 8, C)

    def conv_rows(source, r0, rows, flip):
        acc = jnp.zeros((rows, 2, 8, C), F32)
        for b in range(7):
            for a in range(7):
                k = taps[48 - a * 7 - b] if flip else taps[a * 7 + b]
                acc = acc + source[b, pl.ds(r0 + a, rows)] * k
        return acc

    barrier = pltpu.get_barrier_semaphore()

    def hello(target):
        pl.semaphore_signal(barrier, inc=1, device_id=target, device_id_type=MESH)

    hello(north)

    @pl.when(has_south)
    def _():
        hello(south)
        hello(bot_r)
        hello(bot_l)

    @pl.when(other_r)
    def _():
        hello(top_r)

    @pl.when(other_l)
    def _():
        hello(top_l)

    hello(east)
    hello(west)

    @pl.loop(1, nz)
    def _(d):
        hello(in_z(lax.rem(zi + d, nz)))

    @pl.loop(1, size)
    def _(d):
        hello(in_group(lax.rem(me + d, size)))

    hello(pair)
    for load in loads[3:]:
        load.start()

    by_row = one_hot((CELLS, ROWS), lambda a, b: a // COLS == b)
    by_col = one_hot((CELLS, COLS), lambda a, b: a % COLS == b).astype(F32)

    def pick_cell(a):
        e = (a // 3) * COLS + 13 + a % 3
        w = ((a - 96) // 3) * COLS + (a - 96) % 3
        c, i = (a - 192) // 16, (a - 192) % 16
        corner = (i // 3 + (ROWS - 3) * (c // 2)) * COLS + i % 3 + 13 * (c % 2)
        return jnp.where(a < 96, e, jnp.where(a < 192, w, jnp.where(i < 9, corner, -1)))

    picks = one_hot((256, CELLS), lambda a, b: pick_cell(a) == b)
    left_put = one_hot(
        (ROWS * 8, 96), lambda a, b: (a % 8 >= 5) & ((a // 8) * 3 + a % 8 - 5 == b)
    )
    right_put = one_hot((ROWS * 8, 96), lambda a, b: (a % 8 < 3) & ((a // 8) * 3 + a % 8 == b))

    def put_cell(a, fold):
        m, q = a // WIDE, a % WIDE
        row = jnp.where(fold, 2 - m, m)
        mid = row * COLS + jnp.where(fold, 23 - q, q - 8)
        lo = 48 + row * 3 + jnp.where(fold, 7 - q, q - 5)
        hi = 64 + row * 3 + jnp.where(fold, 26 - q, q - 24)
        hi = jnp.where((q >= 24) & (q < 27), hi, -1)
        return jnp.where((q >= 8) & (q < 24), mid, jnp.where((q >= 5) & (q < 8), lo, hi))

    north_put = one_hot((3 * WIDE, 80), lambda a, b: put_cell(a, is_top) == b)
    south_put = one_hot((3 * WIDE, 80), lambda a, b: put_cell(a, False) == b)

    def halo_copies(n):
        slot = jnp.where(is_top, 0, 1)

        def copy(src, dst, s, r, target):
            return remote("halo", src, dst, halo_s.at[n, s], halo_r.at[n, r], target)

        corner = ksend.at[n]
        return dict(
            e=copy(csend.at[n, 0], crecv.at[n, 0], 0, 0, east),
            w=copy(csend.at[n, 1], crecv.at[n, 1], 1, 1, west),
            up=copy(own_s.at[n, ROWS - 3 : ROWS], vrecv.at[n, slot, 0:3], 2, 2 + slot, north),
            tr=copy(
                corner.at[3],
                vrecv.at[n, slot, 4 - slot],
                3,
                jnp.where(is_top, 5, 6),
                top_r,
            ),
            tl=copy(
                corner.at[2],
                vrecv.at[n, slot, 3 + slot],
                4,
                jnp.where(is_top, 4, 7),
                top_l,
            ),
            down=copy(own_s.at[n, 0:3], vrecv.at[n, 0, 0:3], 5, 2, south),
            br=copy(corner.at[1], vrecv.at[n, 0, 3], 6, 4, bot_r),
            bl=copy(corner.at[0], vrecv.at[n, 0, 4], 7, 5, bot_l),
        )

    def pick_halo(n):
        picked = dot(picks, own_s[n].reshape(CELLS, C)).astype(BF16)
        csend[n] = picked[0:192].reshape(2, 96, C)
        ksend[n] = picked[192:256].reshape(4, 16, C)

    def send_halo(n):
        copies = halo_copies(n)
        copies["up"].start()

        @pl.when(has_south)
        def _():
            copies["down"].start()
            copies["br"].start()
            copies["bl"].start()

        @pl.when(other_r)
        def _():
            copies["tr"].start()

        @pl.when(other_l)
        def _():
            copies["tl"].start()

        copies["e"].start()
        copies["w"].start()

        @pl.when(self_r)
        def _():
            vrecv[n, 0, 4] = ksend[n, 3]

        @pl.when(self_l)
        def _():
            vrecv[n, 0, 3] = ksend[n, 2]

    def take_halo(n, field):
        copies = halo_copies(n)

        def arrive(piece, r):
            remote("halo", piece, piece, halo_s.at[n, 0], halo_r.at[n, r], east).wait_recv()

        copies["e"].wait()
        copies["w"].wait()
        field[3 : 3 + ROWS, 0:8, :] = dot(left_put, crecv[n, 0]).reshape(ROWS, 8, C)
        field[3 : 3 + ROWS, 24:32, :] = dot(right_put, crecv[n, 1]).reshape(ROWS, 8, C)
        copies["up"].wait_send()
        arrive(vrecv.at[n, 0, 0:3], 2)

        @pl.when(other_r)
        def _():
            copies["tr"].wait_send()
            arrive(vrecv.at[n, 0, 4], 5)

        @pl.when(other_l)
        def _():
            copies["tl"].wait_send()
            arrive(vrecv.at[n, 0, 3], 4)

        field[ROWS + 3 : ROWS + 6] = dot(north_put, vrecv[n, 0].reshape(80, C)).reshape(3, WIDE, C)

        @pl.when(has_south)
        def _():
            for name in ("down", "br", "bl"):
                copies[name].wait_send()
            arrive(vrecv.at[n, 1, 0:3], 3)
            arrive(vrecv.at[n, 1, 3], 6)
            arrive(vrecv.at[n, 1, 4], 7)
            field[0:3] = dot(south_put, vrecv[n, 1].reshape(80, C)).reshape(3, WIDE, C)

        @pl.when(jnp.logical_not(has_south))
        def _():
            field[0:3] = jnp.zeros((3, WIDE, C), F32)

    for load in loads[:3]:
        load.wait()
    sea = dot(by_row, mask[...].astype(F32).astype(BF16), ((1,), (1,))) * by_col
    maskb[...] = dot(sea.astype(BF16), jnp.ones((COLS, C), BF16)).reshape(ROWS, COLS, C)
    own = state[...].astype(F32) * maskb[...]
    pad[3 : 3 + ROWS, 8:24, :] = own
    own_s[0] = own.astype(BF16)
    pick_halo(0)
    for a in range(7):
        k7 = kern[a].astype(F32)
        for b in range(7):
            taps[a * 7 + b] = jnp.broadcast_to(k7[b : b + 1], (8, C))
    sums[...] = jnp.zeros_like(sums)
    sumh[...] = jnp.zeros_like(sumh)
    small[...] = jnp.zeros_like(small)
    extra[...] = jnp.zeros_like(extra)

    hellos = 4 + (size - 1) + (nz - 1) + jnp.where(has_south, 3, 0)
    hellos = hellos + jnp.where(other_r, 1, 0) + jnp.where(other_l, 1, 0)
    pl.semaphore_wait(barrier, hellos)
    send_halo(0)
    for load in loads[3:]:
        load.wait()
    take_halo(0, pad)
    shift(pad, shifted)

    block = 8
    cells = block * COLS

    @pl.loop(0, ROWS // block)
    def _(blk):
        r0 = blk * block
        here = pl.ds(pl.multiple_of(r0 * COLS, cells), cells)
        mixed = jnp.concatenate(
            [conv_rows(shifted, r0 + 4 * i, 4, False).reshape(4 * COLS, C) for i in range(block // 4)],
            axis=0,
        )
        average = jnp.sum(mixed, axis=1, keepdims=True) * (1.0 / C)
        centred = mixed - average
        variance = jnp.sum(centred * centred, axis=1, keepdims=True) * (1.0 / C)
        inv_std = lax.rsqrt(variance + EPSILON)
        unit = centred * inv_std
        normed = (unit * gain[...] + nbias[...]).astype(BF16)
        normed_s[here, :] = normed
        pre = dot(normed, w_in[...]) + b_hid[...].reshape(HID)
        square = pre * pre
        t = jnp.tanh(GELU_A * pre * (1.0 + GELU_B * square))
        half = 0.5 * (1.0 + t)
        hidden = (pre * half).astype(BF16)
        hidden_s[here, :] = hidden
        slope = half + pre * (0.5 * GELU_A) * (1.0 - t * t) * (1.0 + 3.0 * GELU_B * square)
        branch = dot(hidden, w_out[...], ((1,), (1,))) + b_out[...]
        rows_here = pl.ds(r0, block)
        sea_w = maskb[rows_here].reshape(cells, C)
        st = state[rows_here].astype(F32).reshape(cells, C)
        ct = cot[rows_here].astype(F32).reshape(cells, C) * sea_w
        block_out[rows_here] = (
            (sea_w * (st + scale[...] * branch)).astype(BF16).reshape(block, COLS, C)
        )
        grad_branch = ct * scale[...]
        bcot = grad_branch.astype(BF16)
        bcot_s[here, :] = bcot
        grad_pre = dot(bcot, w_out[...]) * slope
        precot = grad_pre.astype(BF16)
        precot_s[here, :] = precot
        grad_normed = dot(precot, w_in[...], ((1,), (1,)))
        grad_unit = grad_normed * gain[...]
        mean_a = jnp.sum(grad_unit, axis=1, keepdims=True) * (1.0 / C)
        mean_b = jnp.sum(grad_unit * unit, axis=1, keepdims=True) * (1.0 / C)
        grad_mixed = inv_std * (grad_unit - mean_a - unit * mean_b)
        mcot = grad_mixed.astype(BF16)
        own_s[1, rows_here] = mcot.reshape(block, COLS, C)
        padq[pl.ds(3 + r0, block), 8:24, :] = mcot.astype(F32).reshape(block, COLS, C)

        def fold8(v):
            return jnp.sum(v.reshape(cells // 8, 8, v.shape[1]), axis=0)

        sums[0] += fold8(grad_normed * unit)
        sums[1] += fold8(grad_normed)
        sums[2] += fold8(grad_branch)
        sums[3] += fold8(ct * branch)
        sumh[...] += fold8(grad_pre)

    pick_halo(1)
    send_halo(1)
    block_store = pltpu.make_async_copy(block_out, block_h, store_s.at[0])
    block_store.start()

    for t in range(HID // 256):
        wide = slice(256 * t, 256 * t + 256)
        g_in = dot(normed_s[...], precot_s[:, wide], ((0,), (0,)))
        g_out = dot(bcot_s[...], hidden_s[:, wide], ((0,), (0,)))
        for j in range(2):
            to = slice((2 * t + j) * C, (2 * t + j + 1) * C)
            wbuf[0, to, :] = g_in[:, 128 * j : 128 * j + 128]
            wbuf[1, to, :] = g_out[:, 128 * j : 128 * j + 128]

    def to_pair(i, rows):
        return remote("pair", wbuf.at[1 - core, rows], wrecv.at[rows], core_s.at[i], core_r.at[i], pair)

    pair_w = to_pair(0, pl.ds(0, WROWS))
    pair_w.start()

    for b in range(7):

        def step(i, accs, b=b):
            r0 = i * 4
            m = padq[pl.ds(3 + r0, 4), 8:24, :].reshape(4, 2, 8, C)
            return tuple(
                accs[a] + jnp.sum((m * shifted[b, pl.ds(r0 + a, 4)]).reshape(8, 8, C), axis=0)
                for a in range(7)
            )

        accs = lax.fori_loop(0, ROWS // 4, step, tuple(jnp.zeros((8, C), F32) for _ in range(7)))
        for a in range(7):
            small[a * 7 + b : a * 7 + b + 1, 0:C] = jnp.sum(accs[a], axis=0, keepdims=True)
    for i in range(4):
        small[49 + i : 50 + i, 0:C] = jnp.sum(sums[i], axis=0, keepdims=True)
    hid_row = jnp.sum(sumh[...], axis=0, keepdims=True)
    for i in range(3):
        small[53 + i : 54 + i, :] = hid_row[:, 256 * i : 256 * i + 256]
    wbuf[0, WROWS:, :] = small[:, 0:128]
    wbuf[1, WROWS:, :] = small[:, 128:256]
    pair_s = to_pair(1, pl.ds(WROWS, SROWS))
    pair_s.start()

    pair_w.wait()

    @pl.loop(0, size)
    def _(k):
        rows = pl.ds(pl.multiple_of(k * mrows, 32), mrows)
        both = wbuf[core, rows, :] + wrecv[rows, :]
        psum[rows, :] = both
        pay[k, 0:mrows, :] = both.astype(BF16)

    pair_s.wait()
    rest_w = wbuf[core, MAIN:WROWS, :] + wrecv[MAIN:WROWS, :]
    both = wbuf[core, WROWS:, :] + wrecv[WROWS:, :]
    high = both.astype(BF16).astype(F32)
    other = jnp.concatenate([rest_w, high, both - high], axis=0)
    for i in range((TOT - MAIN) // size):
        extra[pl.ds(i, size, stride=erows), :] = other[i * size : (i + 1) * size]
    pay[:, mrows:, :] = extra[...].reshape(size, erows, 128).astype(BF16)

    def group_copy(k, sender):
        return remote("group", pay.at[k], xrecv.at[sender], xs.at[k], xr.at[sender], in_group(k))

    @pl.loop(1, size)
    def _(d):
        k = lax.rem(me + d, size)
        group_copy(k, me).start()

    def halves(v):
        first = (WROWS - MAIN) // size
        count = SROWS // size
        end = v.shape[0]
        row = lax.broadcasted_iota(jnp.int32, v.shape, 0) - mrows
        whole = v + pltpu.roll(v, end - count, 0)
        top = whole.astype(BF16).astype(F32)
        low = pltpu.roll(whole - top, count, 0)
        is_high = (row >= first) & (row < first + count)
        is_low = (row >= first + count) & (row < first + 2 * count)
        return jnp.where(is_high, top, jnp.where(is_low, low, v)).astype(BF16)

    @pl.loop(1, size)
    def _(d):
        k = lax.rem(me + d, size)
        group_copy(k, k).wait()

    def add_chunk(d, acc):
        return acc + xrecv[lax.rem(me + d, size)].astype(F32)

    mine = jnp.concatenate(
        [
            psum[pl.ds(pl.multiple_of(me * mrows, 32), mrows), :],
            extra[pl.ds(pl.multiple_of(me * erows, 16), erows), :],
        ],
        axis=0,
    )
    zslot[zi] = halves(lax.fori_loop(1, size, add_chunk, mine))

    def z_copy(k, sender):
        return remote("z", zslot.at[sender], zslot.at[sender], zs.at[k], zr.at[sender], in_z(k))

    @pl.loop(1, nz)
    def _(d):
        z_copy(lax.rem(zi + d, nz), zi).start()

    take_halo(1, padq)
    shift(padq, shiftq)

    @pl.loop(0, ROWS // 4)
    def _(i):
        rows_here = pl.ds(i * 4, 4)
        grad = conv_rows(shiftq, i * 4, 4, True).reshape(4, COLS, C)
        grad_state[rows_here] = (
            maskb[rows_here] * (cot[rows_here].astype(F32) + grad)
        ).astype(BF16)

    @pl.when(is_top)
    def _():
        first = ROWS - 4
        acc = conv_rows(shiftq, first, 4, True)
        parts = [acc[i] for i in range(4)]
        for i in range(1, 4):
            for a in range(7 - i, 7):
                for b in range(7):
                    change = taps[a * 7 + b] - taps[48 - a * 7 - b]
                    parts[i] = parts[i] + shiftq[b, first + i + a] * change
        for i in range(1, 4):
            grad_state[first + i] = (
                maskb[first + i] * (cot[first + i].astype(F32) + parts[i].reshape(COLS, C))
            ).astype(BF16)

    grad_store = pltpu.make_async_copy(grad_state, grad_h, store_s.at[1])
    grad_store.start()

    @pl.loop(1, nz)
    def _(d):
        k = lax.rem(zi + d, nz)
        z_copy(k, k).wait()

    whole = zslot[0].astype(F32)
    for k in range(1, nz):
        whole = whole + zslot[k].astype(F32)
    abuf[me] = halves(whole)

    def back_copy(owner, k):
        return remote("back", abuf.at[owner], abuf.at[owner], xas.at[k], xar.at[owner], in_group(k))

    @pl.loop(1, size)
    def _(d):
        back_copy(me, lax.rem(me + d, size)).start()

    @pl.loop(1, size)
    def _(d):
        k = lax.rem(me + d, size)
        back_copy(k, k).wait()

    last = remote("last", abuf, fin, core_s.at[2], core_r.at[2], pair)
    last.start()
    own_store = pltpu.make_async_copy(abuf, total.at[core], store_s.at[2])
    own_store.start()
    last.wait()
    fin_store = pltpu.make_async_copy(fin, total.at[1 - core], store_s.at[3])
    fin_store.start()
    for store in (block_store, grad_store, own_store, fin_store):
        store.wait()


def finish_kernel(
    factor, size, mrows, erows, total_h, block_h, grad_h,
    block_out, grad_out, gk, gg, gb, gw_in, gbh, gw_out, gbo, gls, total, extra, sem,
):
    moves = [
        pltpu.make_async_copy(src, dst, sem.at[i])
        for i, (src, dst) in enumerate(
            ((total_h, total), (block_h, block_out), (grad_h, grad_out))
        )
    ]
    for move in moves:
        move.start()
    moves[0].wait()
    small = []
    for c, gw in ((0, gw_in), (1, gw_out)):
        rows = total[c, :, 0:mrows, :].reshape(MAIN, 128).astype(F32) * factor
        extra[...] = total[c, :, mrows:, :].reshape(size * erows, 128).astype(F32) * factor
        rest = [extra[pl.ds(i, size, stride=erows), :] for i in range((TOT - MAIN) // size)]
        rows = jnp.concatenate([rows] + rest, axis=0)
        for t in range(HID // 128):
            gw[:, 128 * t : 128 * t + 128] = rows[t * C : (t + 1) * C]
        small.append(rows[WROWS : WROWS + SROWS] + rows[WROWS + SROWS :])
    near, far = small
    for a in range(7):
        gk[a, :, 0:128] = near[7 * a : 7 * a + 7]
        gk[a, :, 128:C] = far[7 * a : 7 * a + 7, 0 : C - 128]
    for i, out in enumerate((gg, gb, gbo, gls)):
        out[:, 0:128] = near[49 + i : 50 + i]
        out[:, 128:C] = far[49 + i : 50 + i, 0 : C - 128]
    for i in range(3):
        gbh[256 * i : 256 * i + 128] = near[53 + i]
        gbh[256 * i + 128 : 256 * i + 256] = far[53 + i]
    for move in moves[1:]:
        move.wait()


def on_device(
    nlon,
    nlat,
    state,
    land_mask,
    cotangent,
    kernel,
    norm_gain,
    norm_bias,
    weight_in,
    bias_hidden,
    weight_out,
    bias_out,
    layer_scale,
):
    size, nz, mrows, erows = shares(nlon, nlat)
    hbm = pl.BlockSpec(memory_space=pltpu.HBM)
    vmem = pl.BlockSpec(memory_space=pltpu.VMEM)
    dma = pltpu.SemaphoreType.DMA
    row = lambda v: v.reshape(1, -1)
    block, grad, total = pl.pallas_call(
        functools.partial(main_kernel, nlon, nlat),
        out_shape=(
            jax.ShapeDtypeStruct((ROWS, COLS, C), BF16),
            jax.ShapeDtypeStruct((ROWS, COLS, C), BF16),
            jax.ShapeDtypeStruct((2, size, mrows + erows, 128), BF16),
        ),
        in_specs=[hbm] * 11,
        out_specs=(hbm,) * 3,
        scratch_shapes=[
            pltpu.VMEM((ROWS, COLS, C), BF16),
            pltpu.VMEM((ROWS, COLS, C), BF16),
            pltpu.VMEM((ROWS, COLS, C), BF16),
            pltpu.VMEM((COLS, ROWS), jnp.int32),
            pltpu.VMEM((ROWS, COLS, C), BF16),
            pltpu.VMEM((7, 7, C), BF16),
            pltpu.VMEM((1, C), F32),
            pltpu.VMEM((1, C), F32),
            pltpu.VMEM((C, HID), BF16),
            pltpu.VMEM((HID,), F32),
            pltpu.VMEM((C, HID), BF16),
            pltpu.VMEM((1, C), F32),
            pltpu.VMEM((1, C), F32),
            pltpu.VMEM((PADR, WIDE, C), F32),
            pltpu.VMEM((7, PADR, 2, 8, C), F32),
            pltpu.VMEM((PADR, WIDE, C), F32),
            pltpu.VMEM((7, PADR, 2, 8, C), F32),
            pltpu.VMEM((49, 8, C), F32),
            pltpu.VMEM((ROWS, COLS, C), F32),
            pltpu.VMEM((CELLS, C), BF16),
            pltpu.VMEM((CELLS, HID), BF16),
            pltpu.VMEM((CELLS, HID), BF16),
            pltpu.VMEM((CELLS, C), BF16),
            pltpu.VMEM((2, ROWS, COLS, C), BF16),
            pltpu.VMEM((4, 8, C), F32),
            pltpu.VMEM((8, HID), F32),
            pltpu.VMEM((SROWS, 256), F32),
            pltpu.VMEM((2, 2, 96, C), BF16),
            pltpu.VMEM((2, 4, 16, C), BF16),
            pltpu.VMEM((2, 2, 96, C), BF16),
            pltpu.VMEM((2, 2, 5, 16, C), BF16),
            pltpu.VMEM((2, WROWS + SROWS, 128), F32),
            pltpu.VMEM((WROWS + SROWS, 128), F32),
            pltpu.VMEM((MAIN, 128), F32),
            pltpu.VMEM((size * erows, 128), F32),
            pltpu.VMEM((size, mrows + erows, 128), BF16),
            pltpu.VMEM((size, mrows + erows, 128), BF16),
            pltpu.VMEM((nz, mrows + erows, 128), BF16),
            pltpu.VMEM((size, mrows + erows, 128), BF16),
            pltpu.VMEM((size, mrows + erows, 128), BF16),
            dma((11,)),
            dma((4,)),
            dma((2, 8)),
            dma((2, 8)),
            dma((3,)),
            dma((3,)),
            dma((size,)),
            dma((size,)),
            dma((nz,)),
            dma((nz,)),
            dma((size,)),
            dma((size,)),
        ],
        compiler_params=pltpu.CompilerParams(
            collective_id=0, has_side_effects=True, vmem_limit_bytes=56 * 1024 * 1024
        ),
        name="block",
    )(
        state,
        land_mask.T,
        cotangent,
        kernel,
        row(norm_gain),
        row(norm_bias),
        weight_in,
        bias_hidden,
        weight_out.T,
        row(bias_out),
        row(layer_scale),
    )
    factor = 1.0 / math.sqrt(ROWS * nlat * COLS * nlon)
    shape = lambda *s: jax.ShapeDtypeStruct(s, F32)
    outs = pl.pallas_call(
        functools.partial(finish_kernel, factor, size, mrows, erows),
        out_shape=(
            jax.ShapeDtypeStruct((ROWS, COLS, C), BF16),
            jax.ShapeDtypeStruct((ROWS, COLS, C), BF16),
            shape(7, 7, C),
            shape(1, C),
            shape(1, C),
            shape(C, HID),
            shape(HID),
            shape(C, HID),
            shape(1, C),
            shape(1, C),
        ),
        in_specs=[hbm] * 3,
        out_specs=(vmem,) * 10,
        scratch_shapes=[
            pltpu.VMEM((2, size, mrows + erows, 128), BF16),
            pltpu.VMEM((size * erows, 128), F32),
            dma((3,)),
        ],
        compiler_params=pltpu.CompilerParams(vmem_limit_bytes=56 * 1024 * 1024),
        name="finish",
    )(total, block, grad)
    outs = [o.reshape(-1) if o.shape[0] == 1 else o for o in outs]
    outs[7] = outs[7].T
    return tuple(outs)


def solution(mesh):
    cells, plane, whole = P("lat", "lon", None), P("lat", "lon"), P()
    return jax.shard_map(
        functools.partial(on_device, mesh.shape["lon"], mesh.shape["lat"]),
        mesh=mesh,
        in_specs=(cells, plane, cells) + (whole,) * 8,
        out_specs=(cells, cells) + (whole,) * 8,
        check_vma=False,
    )
```

```python
import functools
import math

import jax
import jax.numpy as jnp
from jax import lax
from jax.experimental import pallas as pl
from jax.experimental.pallas import tpu as pltpu
from jax.sharding import PartitionSpec as P

EPSILON = 1e-06
MESH = pl.DeviceIdType.MESH
F32 = jnp.float32
BF16 = jnp.bfloat16

ROWS, COLS, C, HID = 32, 16, 192, 768
CELLS = ROWS * COLS
PADR, WIDE = ROWS + 6, 32
WROWS = C * HID // 128
SROWS = 64
TOT = WROWS + 2 * SROWS
MAIN = 1024
GELU_A = math.sqrt(2.0 / math.pi)
GELU_B = 0.044715


def groups(nlon, nlat):
    px = 4 if nlon >= 64 else 1
    nzl = nlon // (2 * px)
    nzh = 2 if nlat >= 8 else 1
    return px, nzl, nzh, nlat // nzh


def shares(nlon, nlat):
    px, nzl, nzh, py = groups(nlon, nlat)
    size = px * py * 2
    return size, nzl * nzh // 2, MAIN // size, max(16, (TOT - MAIN) // size)


def one_hot(shape, pick):
    a = lax.broadcasted_iota(jnp.int32, shape, 0)
    b = lax.broadcasted_iota(jnp.int32, shape, 1)
    return pick(a, b).astype(F32).astype(BF16)


def dot(a, b, contract=((1,), (0,))):
    return lax.dot_general(a, b, (contract, ((), ())), preferred_element_type=F32)


def remote(kind, src, dst, send, recv, target):
    return pltpu.make_async_remote_copy(
        src_ref=src,
        dst_ref=dst,
        send_sem=send,
        recv_sem=recv,
        device_id=target,
        device_id_type=MESH,
    )


def main_kernel(
    nlon,
    nlat,
    state_h,
    mask_h,
    cot_h,
    kern_h,
    gain_h,
    nbias_h,
    w_in_h,
    b_hid_h,
    w_out_h,
    b_out_h,
    scale_h,
    block_h,
    grad_h,
    total,
    block_out,
    grad_state,
    state,
    mask,
    cot,
    kern,
    gain,
    nbias,
    w_in,
    b_hid,
    w_out,
    b_out,
    scale,
    pad,
    shifted,
    padq,
    shiftq,
    taps,
    maskb,
    mixp,
    ghid_s,
    normed_s,
    precot_s,
    hidden_s,
    bcot_s,
    own_s,
    sums,
    sumh,
    small,
    csend,
    ksend,
    crecv,
    vrecv,
    wbuf,
    wrecv,
    psum,
    extra,
    pay,
    xrecv,
    payx,
    xrecvx,
    zslot,
    abuf,
    fin,
    load_s,
    store_s,
    halo_s,
    halo_r,
    core_s,
    core_r,
    xs,
    xr,
    xsx,
    xrx,
    zs,
    zr,
    xas,
    xar,
    ls,
    lr,
):
    px, nzl, nzh, py = groups(nlon, nlat)
    size, nz, mrows, erows = shares(nlon, nlat)

    loads = [
        pltpu.make_async_copy(src, dst, load_s.at[i])
        for i, (src, dst) in enumerate(
            (
                (state_h, state),
                (mask_h, mask),
                (kern_h, kern),
                (cot_h, cot),
                (w_in_h, w_in),
                (w_out_h, w_out),
                (gain_h, gain),
                (nbias_h, nbias),
                (b_hid_h, b_hid),
                (b_out_h, b_out),
                (scale_h, scale),
            )
        )
    ]
    for load in loads[:3]:
        load.start()

    lon = lax.axis_index("lon")
    lat = lax.axis_index("lat")
    core = lax.rem(lon, 2)
    x = lax.rem(lax.div(lon, 2), px)
    zl = lax.div(lon, 2 * px)
    zh = lax.rem(lat, nzh)
    y = lax.div(lat, nzh)
    odd = lax.rem(zl, 2)
    me = (y * px + x) * 2 + odd
    zi = zh * (nzl // 2) + lax.div(zl, 2)
    is_top = lat == nlat - 1
    has_south = lat > 0

    def device(la, lo):
        return {"lon": lo, "lat": la}

    right, left = lax.rem(lon + 1, nlon), lax.rem(lon + nlon - 1, nlon)
    above, below = jnp.where(is_top, lat, lat + 1), jnp.where(has_south, lat - 1, 0)
    fold_r, fold_l = lax.rem(2 * nlon - 2 - lon, nlon), lax.rem(nlon - lon, nlon)
    east, west = device(lat, right), device(lat, left)
    north = device(above, jnp.where(is_top, nlon - 1 - lon, lon))
    south = device(below, lon)
    top_r = device(above, jnp.where(is_top, fold_r, right))
    top_l = device(above, jnp.where(is_top, fold_l, left))
    bot_r, bot_l = device(below, right), device(below, left)
    self_r = jnp.logical_and(is_top, fold_r == lon)
    self_l = jnp.logical_and(is_top, fold_l == lon)
    other_r, other_l = jnp.logical_not(self_r), jnp.logical_not(self_l)
    pair = device(lat, lon + 1 - 2 * core)

    def in_group(k):
        p = lax.div(k, 2)
        z = zl - odd + lax.rem(k, 2)
        return device(lax.div(p, px) * nzh + zh, z * (2 * px) + lax.rem(p, px) * 2 + core)

    def in_z(k):
        z = lax.rem(k, nzl // 2) * 2 + odd
        return device(y * nzh + lax.div(k, nzl // 2), z * (2 * px) + x * 2 + core)

    def shift(field, out):
        @pl.loop(0, PADR)
        def _(r):
            for b in range(7):
                out[b, r] = field[r, 5 + b : 21 + b, :].reshape(2, 8, C)

    def inner(b, h):
        return b >= 3 if h == 0 else b <= 3

    def shift_some(r, wanted):
        for b in range(7):
            for h in range(2):
                if wanted(b, h):
                    shifted[b, r, h] = pad[r, 5 + b + 8 * h : 13 + b + 8 * h, :]

    def conv_half(r0, h, wanted, acc):
        for b in range(7):
            for a in range(7):
                if wanted(b, h):
                    acc = acc + shifted[b, pl.ds(r0 + a, 4), h] * taps[a * 7 + b]
        return acc

    def conv_inner(r0):
        for h in range(2):
            mixp[pl.ds(r0, 4), h] = conv_half(r0, h, inner, jnp.zeros((4, 8, C), F32))

    def conv_outer(r0):
        halves = [
            conv_half(r0, h, lambda b, h: not inner(b, h), mixp[pl.ds(r0, 4), h]) for h in range(2)
        ]
        return jnp.stack(halves, axis=1).reshape(4 * COLS, C)

    def conv_rows(source, r0, rows, flip):
        acc = jnp.zeros((rows, 2, 8, C), F32)
        for b in range(7):
            for a in range(7):
                k = taps[48 - a * 7 - b] if flip else taps[a * 7 + b]
                acc = acc + source[b, pl.ds(r0 + a, rows)] * k
        return acc

    barrier = pltpu.get_barrier_semaphore()

    def hello(target):
        pl.semaphore_signal(barrier, inc=1, device_id=target, device_id_type=MESH)

    hello(north)

    @pl.when(has_south)
    def _():
        hello(south)
        hello(bot_r)
        hello(bot_l)

    @pl.when(other_r)
    def _():
        hello(top_r)

    @pl.when(other_l)
    def _():
        hello(top_l)

    hello(east)
    hello(west)

    @pl.loop(1, nz)
    def _(d):
        hello(in_z(lax.rem(zi + d, nz)))

    @pl.loop(1, size)
    def _(d):
        hello(in_group(lax.rem(me + d, size)))

    hello(pair)
    for load in loads[3:]:
        load.start()

    by_row = one_hot((CELLS, ROWS), lambda a, b: a // COLS == b)
    by_col = one_hot((CELLS, COLS), lambda a, b: a % COLS == b).astype(F32)

    def pick_cell(a):
        e = (a // 3) * COLS + 13 + a % 3
        w = ((a - 96) // 3) * COLS + (a - 96) % 3
        c, i = (a - 192) // 16, (a - 192) % 16
        corner = (i // 3 + (ROWS - 3) * (c // 2)) * COLS + i % 3 + 13 * (c % 2)
        return jnp.where(a < 96, e, jnp.where(a < 192, w, jnp.where(i < 9, corner, -1)))

    picks = one_hot((256, CELLS), lambda a, b: pick_cell(a) == b)
    left_put = one_hot(
        (ROWS * 8, 96), lambda a, b: (a % 8 >= 5) & ((a // 8) * 3 + a % 8 - 5 == b)
    )
    right_put = one_hot((ROWS * 8, 96), lambda a, b: (a % 8 < 3) & ((a // 8) * 3 + a % 8 == b))

    def put_cell(a, fold):
        m, q = a // WIDE, a % WIDE
        row = jnp.where(fold, 2 - m, m)
        mid = row * COLS + jnp.where(fold, 23 - q, q - 8)
        lo = 48 + row * 3 + jnp.where(fold, 7 - q, q - 5)
        hi = 64 + row * 3 + jnp.where(fold, 26 - q, q - 24)
        hi = jnp.where((q >= 24) & (q < 27), hi, -1)
        return jnp.where((q >= 8) & (q < 24), mid, jnp.where((q >= 5) & (q < 8), lo, hi))

    north_put = one_hot((3 * WIDE, 80), lambda a, b: put_cell(a, is_top) == b)
    south_put = one_hot((3 * WIDE, 80), lambda a, b: put_cell(a, False) == b)

    def halo_copies(n):
        slot = jnp.where(is_top, 0, 1)

        def copy(src, dst, s, r, target):
            return remote("halo", src, dst, halo_s.at[n, s], halo_r.at[n, r], target)

        corner = ksend.at[n]
        return dict(
            e=copy(csend.at[n, 0], crecv.at[n, 0], 0, 0, east),
            w=copy(csend.at[n, 1], crecv.at[n, 1], 1, 1, west),
            up=copy(own_s.at[n, ROWS - 3 : ROWS], vrecv.at[n, slot, 0:3], 2, 2 + slot, north),
            tr=copy(
                corner.at[3],
                vrecv.at[n, slot, 4 - slot],
                3,
                jnp.where(is_top, 5, 6),
                top_r,
            ),
            tl=copy(
                corner.at[2],
                vrecv.at[n, slot, 3 + slot],
                4,
                jnp.where(is_top, 4, 7),
                top_l,
            ),
            down=copy(own_s.at[n, 0:3], vrecv.at[n, 0, 0:3], 5, 2, south),
            br=copy(corner.at[1], vrecv.at[n, 0, 3], 6, 4, bot_r),
            bl=copy(corner.at[0], vrecv.at[n, 0, 4], 7, 5, bot_l),
        )

    def pick_halo(n):
        picked = dot(picks, own_s[n].reshape(CELLS, C)).astype(BF16)
        csend[n] = picked[0:192].reshape(2, 96, C)
        ksend[n] = picked[192:256].reshape(4, 16, C)

    def send_halo(n):
        copies = halo_copies(n)
        copies["up"].start()

        @pl.when(has_south)
        def _():
            copies["down"].start()
            copies["br"].start()
            copies["bl"].start()

        @pl.when(other_r)
        def _():
            copies["tr"].start()

        @pl.when(other_l)
        def _():
            copies["tl"].start()

        copies["e"].start()
        copies["w"].start()

        @pl.when(self_r)
        def _():
            vrecv[n, 0, 4] = ksend[n, 3]

        @pl.when(self_l)
        def _():
            vrecv[n, 0, 3] = ksend[n, 2]

    def take_halo(n, field):
        copies = halo_copies(n)

        def arrive(piece, r):
            remote("halo", piece, piece, halo_s.at[n, 0], halo_r.at[n, r], east).wait_recv()

        copies["e"].wait()
        copies["w"].wait()
        field[3 : 3 + ROWS, 0:8, :] = dot(left_put, crecv[n, 0]).reshape(ROWS, 8, C)
        field[3 : 3 + ROWS, 24:32, :] = dot(right_put, crecv[n, 1]).reshape(ROWS, 8, C)
        copies["up"].wait_send()
        arrive(vrecv.at[n, 0, 0:3], 2)

        @pl.when(other_r)
        def _():
            copies["tr"].wait_send()
            arrive(vrecv.at[n, 0, 4], 5)

        @pl.when(other_l)
        def _():
            copies["tl"].wait_send()
            arrive(vrecv.at[n, 0, 3], 4)

        field[ROWS + 3 : ROWS + 6] = dot(north_put, vrecv[n, 0].reshape(80, C)).reshape(3, WIDE, C)

        @pl.when(has_south)
        def _():
            for name in ("down", "br", "bl"):
                copies[name].wait_send()
            arrive(vrecv.at[n, 1, 0:3], 3)
            arrive(vrecv.at[n, 1, 3], 6)
            arrive(vrecv.at[n, 1, 4], 7)
            field[0:3] = dot(south_put, vrecv[n, 1].reshape(80, C)).reshape(3, WIDE, C)

        @pl.when(jnp.logical_not(has_south))
        def _():
            field[0:3] = jnp.zeros((3, WIDE, C), F32)

    for load in loads[:3]:
        load.wait()
    sea = dot(by_row, mask[...].astype(F32).astype(BF16), ((1,), (1,))) * by_col
    maskb[...] = dot(sea.astype(BF16), jnp.ones((COLS, C), BF16)).reshape(ROWS, COLS, C)
    own = state[...].astype(F32) * maskb[...]
    pad[3 : 3 + ROWS, 8:24, :] = own
    own_s[0] = own.astype(BF16)
    pick_halo(0)
    for a in range(7):
        k7 = kern[a].astype(F32)
        for b in range(7):
            taps[a * 7 + b] = jnp.broadcast_to(k7[b : b + 1], (8, C))
    sums[...] = jnp.zeros_like(sums)
    sumh[...] = jnp.zeros_like(sumh)
    small[...] = jnp.zeros_like(small)
    extra[...] = jnp.zeros_like(extra)

    hellos = 4 + (size - 1) + (nz - 1) + jnp.where(has_south, 3, 0)
    hellos = hellos + jnp.where(other_r, 1, 0) + jnp.where(other_l, 1, 0)
    pl.semaphore_wait(barrier, hellos)
    send_halo(0)
    for load in loads[3:]:
        load.wait()

    ct_all = cot[...].astype(F32) * maskb[...]
    gb_all = (ct_all * scale[...].reshape(1, 1, C)).reshape(CELLS, C)
    bcot_s[...] = gb_all.astype(BF16)
    sums[2] = jnp.sum(gb_all.reshape(CELLS // 8, 8, C), axis=0)
    for t in range(HID // 256):
        wide = slice(256 * t, 256 * t + 256)
        ghid_s[:, wide] = dot(bcot_s[...], w_out[:, wide])

    @pl.loop(3, 3 + ROWS)
    def _(r):
        shift_some(r, inner)

    @pl.loop(1, ROWS // 4 - 1)
    def _(i):
        conv_inner(4 * i)

    take_halo(0, pad)

    @pl.loop(3, 3 + ROWS)
    def _(r):
        shift_some(r, lambda b, h: not inner(b, h))

    for q in range(3):
        shift_some(q, lambda b, h: True)
        shift_some(ROWS + 3 + q, lambda b, h: True)
    conv_inner(0)
    conv_inner(ROWS - 4)

    block = 8
    cells = block * COLS

    @pl.loop(0, ROWS // block)
    def _(blk):
        r0 = blk * block
        here = pl.ds(pl.multiple_of(r0 * COLS, cells), cells)
        mixed = jnp.concatenate(
            [conv_outer(r0 + 4 * i) for i in range(block // 4)],
            axis=0,
        )
        average = jnp.sum(mixed, axis=1, keepdims=True) * (1.0 / C)
        centred = mixed - average
        variance = jnp.sum(centred * centred, axis=1, keepdims=True) * (1.0 / C)
        inv_std = lax.rsqrt(variance + EPSILON)
        unit = centred * inv_std
        normed = (unit * gain[...] + nbias[...]).astype(BF16)
        normed_s[here, :] = normed
        pre = dot(normed, w_in[...]) + b_hid[...].reshape(HID)
        square = pre * pre
        t = jnp.tanh(GELU_A * pre * (1.0 + GELU_B * square))
        half = 0.5 * (1.0 + t)
        hidden = (pre * half).astype(BF16)
        hidden_s[here, :] = hidden
        slope = half + pre * (0.5 * GELU_A) * (1.0 - t * t) * (1.0 + 3.0 * GELU_B * square)
        branch = dot(hidden, w_out[...], ((1,), (1,))) + b_out[...]
        rows_here = pl.ds(r0, block)
        sea_w = maskb[rows_here].reshape(cells, C)
        st = state[rows_here].astype(F32).reshape(cells, C)
        ct = cot[rows_here].astype(F32).reshape(cells, C) * sea_w
        block_out[rows_here] = (
            (sea_w * (st + scale[...] * branch)).astype(BF16).reshape(block, COLS, C)
        )
        grad_pre = ghid_s[here, :] * slope
        precot = grad_pre.astype(BF16)
        precot_s[here, :] = precot
        grad_normed = dot(precot, w_in[...], ((1,), (1,)))
        grad_unit = grad_normed * gain[...]
        mean_a = jnp.sum(grad_unit, axis=1, keepdims=True) * (1.0 / C)
        mean_b = jnp.sum(grad_unit * unit, axis=1, keepdims=True) * (1.0 / C)
        grad_mixed = inv_std * (grad_unit - mean_a - unit * mean_b)
        mcot = grad_mixed.astype(BF16)
        own_s[1, rows_here] = mcot.reshape(block, COLS, C)
        padq[pl.ds(3 + r0, block), 8:24, :] = mcot.astype(F32).reshape(block, COLS, C)

        def fold8(v):
            return jnp.sum(v.reshape(cells // 8, 8, v.shape[1]), axis=0)

        sums[0] += fold8(grad_normed * unit)
        sums[1] += fold8(grad_normed)
        sums[3] += fold8(ct * branch)
        sumh[...] += fold8(grad_pre)

    pick_halo(1)
    send_halo(1)
    block_store = pltpu.make_async_copy(block_out, block_h, store_s.at[0])
    block_store.start()

    for t in range(HID // 256):
        wide = slice(256 * t, 256 * t + 256)
        g_in = dot(normed_s[...], precot_s[:, wide], ((0,), (0,)))
        g_out = dot(bcot_s[...], hidden_s[:, wide], ((0,), (0,)))
        for j in range(2):
            to = slice((2 * t + j) * C, (2 * t + j + 1) * C)
            wbuf[0, to, :] = g_in[:, 128 * j : 128 * j + 128]
            wbuf[1, to, :] = g_out[:, 128 * j : 128 * j + 128]

    def to_pair(i, rows):
        return remote("pair", wbuf.at[1 - core, rows], wrecv.at[rows], core_s.at[i], core_r.at[i], pair)

    pair_w = to_pair(0, pl.ds(0, WROWS))
    pair_w.start()

    def kernel_grad(b):
        def step(i, accs):
            r0 = i * 4
            m = padq[pl.ds(3 + r0, 4), 8:24, :].reshape(4, 2, 8, C)
            return tuple(
                accs[a] + jnp.sum((m * shifted[b, pl.ds(r0 + a, 4)]).reshape(8, 8, C), axis=0)
                for a in range(7)
            )

        accs = lax.fori_loop(0, ROWS // 4, step, tuple(jnp.zeros((8, C), F32) for _ in range(7)))
        for a in range(7):
            small[a * 7 + b : a * 7 + b + 1, 0:C] = jnp.sum(accs[a], axis=0, keepdims=True)

    for b in range(3):
        kernel_grad(b)

    def group_copy(k, sender):
        return remote("group", pay.at[k], xrecv.at[sender], xs.at[k], xr.at[sender], in_group(k))

    def rest_copy(k, sender):
        return remote("group", payx.at[k], xrecvx.at[sender], xsx.at[k], xrx.at[sender], in_group(k))

    pair_w.wait()

    def add_pair(k):
        rows = pl.ds(pl.multiple_of(k * mrows, 32), mrows)
        both = wbuf[core, rows, :] + wrecv[rows, :]
        psum[rows, :] = both
        pay[k] = both.astype(BF16)

    add_pair(me)

    @pl.loop(1, size)
    def _(d):
        k = lax.rem(me + d, size)
        add_pair(k)
        group_copy(k, me).start()

    for b in range(3, 7):
        kernel_grad(b)
    for i in range(4):
        small[49 + i : 50 + i, 0:C] = jnp.sum(sums[i], axis=0, keepdims=True)
    hid_row = jnp.sum(sumh[...], axis=0, keepdims=True)
    for i in range(3):
        small[53 + i : 54 + i, :] = hid_row[:, 256 * i : 256 * i + 256]
    wbuf[0, WROWS:, :] = small[:, 0:128]
    wbuf[1, WROWS:, :] = small[:, 128:256]
    pair_s = to_pair(1, pl.ds(WROWS, SROWS))
    pair_s.start()

    pair_s.wait()
    rest_w = wbuf[core, MAIN:WROWS, :] + wrecv[MAIN:WROWS, :]
    both = wbuf[core, WROWS:, :] + wrecv[WROWS:, :]
    high = both.astype(BF16).astype(F32)
    other = jnp.concatenate([rest_w, high, both - high], axis=0)
    for i in range((TOT - MAIN) // size):
        extra[pl.ds(i, size, stride=erows), :] = other[i * size : (i + 1) * size]
    payx[...] = extra[...].reshape(size, erows, 128).astype(BF16)

    @pl.loop(1, size)
    def _(d):
        k = lax.rem(me + d, size)
        rest_copy(k, me).start()

    def halves(v):
        first = (WROWS - MAIN) // size
        count = SROWS // size
        end = v.shape[0]
        row = lax.broadcasted_iota(jnp.int32, v.shape, 0) - mrows
        whole = v + pltpu.roll(v, end - count, 0)
        top = whole.astype(BF16).astype(F32)
        low = pltpu.roll(whole - top, count, 0)
        is_high = (row >= first) & (row < first + count)
        is_low = (row >= first + count) & (row < first + 2 * count)
        return jnp.where(is_high, top, jnp.where(is_low, low, v)).astype(BF16)

    @pl.loop(1, size)
    def _(d):
        k = lax.rem(me + d, size)
        group_copy(k, k).wait()

    def add_main(d, acc):
        return acc + xrecv[lax.rem(me + d, size)].astype(F32)

    def add_rest(d, acc):
        return acc + xrecvx[lax.rem(me + d, size)].astype(F32)

    mine = psum[pl.ds(pl.multiple_of(me * mrows, 32), mrows), :]
    mine = lax.fori_loop(1, size, add_main, mine)

    @pl.loop(1, size)
    def _(d):
        k = lax.rem(me + d, size)
        rest_copy(k, k).wait()

    minex = extra[pl.ds(pl.multiple_of(me * erows, 16), erows), :]
    minex = lax.fori_loop(1, size, add_rest, minex)
    zslot[zi] = halves(jnp.concatenate([mine, minex], axis=0))

    def z_copy(k, sender):
        return remote("z", zslot.at[sender], zslot.at[sender], zs.at[k], zr.at[sender], in_z(k))

    @pl.loop(1, nz)
    def _(d):
        z_copy(lax.rem(zi + d, nz), zi).start()

    take_halo(1, padq)
    shift(padq, shiftq)

    @pl.loop(0, ROWS // 4)
    def _(i):
        rows_here = pl.ds(i * 4, 4)
        grad = conv_rows(shiftq, i * 4, 4, True).reshape(4, COLS, C)
        grad_state[rows_here] = (
            maskb[rows_here] * (cot[rows_here].astype(F32) + grad)
        ).astype(BF16)

    @pl.when(is_top)
    def _():
        first = ROWS - 4
        acc = conv_rows(shiftq, first, 4, True)
        parts = [acc[i] for i in range(4)]
        for i in range(1, 4):
            for a in range(7 - i, 7):
                for b in range(7):
                    change = taps[a * 7 + b] - taps[48 - a * 7 - b]
                    parts[i] = parts[i] + shiftq[b, first + i + a] * change
        for i in range(1, 4):
            grad_state[first + i] = (
                maskb[first + i] * (cot[first + i].astype(F32) + parts[i].reshape(COLS, C))
            ).astype(BF16)

    grad_store = pltpu.make_async_copy(grad_state, grad_h, store_s.at[1])
    grad_store.start()

    @pl.loop(1, nz)
    def _(d):
        k = lax.rem(zi + d, nz)
        z_copy(k, k).wait()

    whole = zslot[0].astype(F32)
    for k in range(1, nz):
        whole = whole + zslot[k].astype(F32)
    abuf[me] = halves(whole)

    def back_copy(owner, k):
        return remote("back", abuf.at[owner], abuf.at[owner], xas.at[k], xar.at[owner], in_group(k))

    @pl.loop(1, size)
    def _(d):
        back_copy(me, lax.rem(me + d, size)).start()

    def last_copy(k):
        return remote("last", abuf.at[k], fin.at[k], ls.at[k], lr.at[k], pair)

    last_copy(me).start()

    @pl.loop(1, size)
    def _(d):
        k = lax.rem(me + d, size)
        back_copy(k, k).wait()
        last_copy(k).start()

    own_store = pltpu.make_async_copy(abuf, total.at[core], store_s.at[2])
    own_store.start()

    @pl.loop(0, size)
    def _(k):
        last_copy(k).wait()

    fin_store = pltpu.make_async_copy(fin, total.at[1 - core], store_s.at[3])
    fin_store.start()
    for store in (block_store, grad_store, own_store, fin_store):
        store.wait()


def finish_kernel(
    factor, size, mrows, erows, total_h, block_h, grad_h,
    block_out, grad_out, gk, gg, gb, gw_in, gbh, gw_out, gbo, gls, total, extra, sem,
):
    moves = [
        pltpu.make_async_copy(src, dst, sem.at[i])
        for i, (src, dst) in enumerate(
            ((total_h, total), (block_h, block_out), (grad_h, grad_out))
        )
    ]
    for move in moves:
        move.start()
    moves[0].wait()
    small = []
    for c, gw in ((0, gw_in), (1, gw_out)):
        rows = total[c, :, 0:mrows, :].reshape(MAIN, 128).astype(F32) * factor
        extra[...] = total[c, :, mrows:, :].reshape(size * erows, 128).astype(F32) * factor
        rest = [extra[pl.ds(i, size, stride=erows), :] for i in range((TOT - MAIN) // size)]
        rows = jnp.concatenate([rows] + rest, axis=0)
        for t in range(HID // 128):
            gw[:, 128 * t : 128 * t + 128] = rows[t * C : (t + 1) * C]
        small.append(rows[WROWS : WROWS + SROWS] + rows[WROWS + SROWS :])
    near, far = small
    for a in range(7):
        gk[a, :, 0:128] = near[7 * a : 7 * a + 7]
        gk[a, :, 128:C] = far[7 * a : 7 * a + 7, 0 : C - 128]
    for i, out in enumerate((gg, gb, gbo, gls)):
        out[:, 0:128] = near[49 + i : 50 + i]
        out[:, 128:C] = far[49 + i : 50 + i, 0 : C - 128]
    for i in range(3):
        gbh[256 * i : 256 * i + 128] = near[53 + i]
        gbh[256 * i + 128 : 256 * i + 256] = far[53 + i]
    for move in moves[1:]:
        move.wait()


def on_device(
    nlon,
    nlat,
    state,
    land_mask,
    cotangent,
    kernel,
    norm_gain,
    norm_bias,
    weight_in,
    bias_hidden,
    weight_out,
    bias_out,
    layer_scale,
):
    size, nz, mrows, erows = shares(nlon, nlat)
    hbm = pl.BlockSpec(memory_space=pltpu.HBM)
    vmem = pl.BlockSpec(memory_space=pltpu.VMEM)
    dma = pltpu.SemaphoreType.DMA
    row = lambda v: v.reshape(1, -1)
    block, grad, total = pl.pallas_call(
        functools.partial(main_kernel, nlon, nlat),
        out_shape=(
            jax.ShapeDtypeStruct((ROWS, COLS, C), BF16),
            jax.ShapeDtypeStruct((ROWS, COLS, C), BF16),
            jax.ShapeDtypeStruct((2, size, mrows + erows, 128), BF16),
        ),
        in_specs=[hbm] * 11,
        out_specs=(hbm,) * 3,
        scratch_shapes=[
            pltpu.VMEM((ROWS, COLS, C), BF16),
            pltpu.VMEM((ROWS, COLS, C), BF16),
            pltpu.VMEM((ROWS, COLS, C), BF16),
            pltpu.VMEM((COLS, ROWS), jnp.int32),
            pltpu.VMEM((ROWS, COLS, C), BF16),
            pltpu.VMEM((7, 7, C), BF16),
            pltpu.VMEM((1, C), F32),
            pltpu.VMEM((1, C), F32),
            pltpu.VMEM((C, HID), BF16),
            pltpu.VMEM((HID,), F32),
            pltpu.VMEM((C, HID), BF16),
            pltpu.VMEM((1, C), F32),
            pltpu.VMEM((1, C), F32),
            pltpu.VMEM((PADR, WIDE, C), F32),
            pltpu.VMEM((7, PADR, 2, 8, C), F32),
            pltpu.VMEM((PADR, WIDE, C), F32),
            pltpu.VMEM((7, PADR, 2, 8, C), F32),
            pltpu.VMEM((49, 8, C), F32),
            pltpu.VMEM((ROWS, COLS, C), F32),
            pltpu.VMEM((ROWS, 2, 8, C), F32),
            pltpu.VMEM((CELLS, HID), F32),
            pltpu.VMEM((CELLS, C), BF16),
            pltpu.VMEM((CELLS, HID), BF16),
            pltpu.VMEM((CELLS, HID), BF16),
            pltpu.VMEM((CELLS, C), BF16),
            pltpu.VMEM((2, ROWS, COLS, C), BF16),
            pltpu.VMEM((4, 8, C), F32),
            pltpu.VMEM((8, HID), F32),
            pltpu.VMEM((SROWS, 256), F32),
            pltpu.VMEM((2, 2, 96, C), BF16),
            pltpu.VMEM((2, 4, 16, C), BF16),
            pltpu.VMEM((2, 2, 96, C), BF16),
            pltpu.VMEM((2, 2, 5, 16, C), BF16),
            pltpu.VMEM((2, WROWS + SROWS, 128), F32),
            pltpu.VMEM((WROWS + SROWS, 128), F32),
            pltpu.VMEM((MAIN, 128), F32),
            pltpu.VMEM((size * erows, 128), F32),
            pltpu.VMEM((size, mrows, 128), BF16),
            pltpu.VMEM((size, mrows, 128), BF16),
            pltpu.VMEM((size, erows, 128), BF16),
            pltpu.VMEM((size, erows, 128), BF16),
            pltpu.VMEM((nz, mrows + erows, 128), BF16),
            pltpu.VMEM((size, mrows + erows, 128), BF16),
            pltpu.VMEM((size, mrows + erows, 128), BF16),
            dma((11,)),
            dma((4,)),
            dma((2, 8)),
            dma((2, 8)),
            dma((2,)),
            dma((2,)),
            dma((size,)),
            dma((size,)),
            dma((size,)),
            dma((size,)),
            dma((nz,)),
            dma((nz,)),
            dma((size,)),
            dma((size,)),
            dma((size,)),
            dma((size,)),
        ],
        compiler_params=pltpu.CompilerParams(
            collective_id=0, has_side_effects=True, vmem_limit_bytes=56 * 1024 * 1024
        ),
        name="block",
    )(
        state,
        land_mask.T,
        cotangent,
        kernel,
        row(norm_gain),
        row(norm_bias),
        weight_in,
        bias_hidden,
        weight_out.T,
        row(bias_out),
        row(layer_scale),
    )
    factor = 1.0 / math.sqrt(ROWS * nlat * COLS * nlon)
    shape = lambda *s: jax.ShapeDtypeStruct(s, F32)
    outs = pl.pallas_call(
        functools.partial(finish_kernel, factor, size, mrows, erows),
        out_shape=(
            jax.ShapeDtypeStruct((ROWS, COLS, C), BF16),
            jax.ShapeDtypeStruct((ROWS, COLS, C), BF16),
            shape(7, 7, C),
            shape(1, C),
            shape(1, C),
            shape(C, HID),
            shape(HID),
            shape(C, HID),
            shape(1, C),
            shape(1, C),
        ),
        in_specs=[hbm] * 3,
        out_specs=(vmem,) * 10,
        scratch_shapes=[
            pltpu.VMEM((2, size, mrows + erows, 128), BF16),
            pltpu.VMEM((size * erows, 128), F32),
            dma((3,)),
        ],
        compiler_params=pltpu.CompilerParams(vmem_limit_bytes=56 * 1024 * 1024),
        name="finish",
    )(total, block, grad)
    outs = [o.reshape(-1) if o.shape[0] == 1 else o for o in outs]
    outs[7] = outs[7].T
    return tuple(outs)


def solution(mesh):
    cells, plane, whole = P("lat", "lon", None), P("lat", "lon"), P()
    return jax.shard_map(
        functools.partial(on_device, mesh.shape["lon"], mesh.shape["lat"]),
        mesh=mesh,
        in_specs=(cells, plane, cells) + (whole,) * 8,
        out_specs=(cells, cells) + (whole,) * 8,
        check_vma=False,
    )
```

```python
import functools
import math

import jax
import jax.numpy as jnp
from jax import lax
from jax.experimental import pallas as pl
from jax.experimental.pallas import tpu as pltpu
from jax.sharding import PartitionSpec as P

EPSILON = 1e-06
MESH = pl.DeviceIdType.MESH
F32 = jnp.float32
BF16 = jnp.bfloat16

ROWS, COLS, C, HID = 32, 16, 192, 768
CELLS = ROWS * COLS
PADR, WIDE = ROWS + 6, 32
WROWS = C * HID // 128
SROWS = 64
TOT = WROWS + 2 * SROWS
MAIN = 1024
GELU_A = math.sqrt(2.0 / math.pi)
GELU_B = 0.044715


def groups(nlon, nlat):
    px = 4 if nlon >= 64 else 1
    nzl = nlon // (2 * px)
    nzh = 2 if nlat >= 8 else 1
    return px, nzl, nzh, nlat // nzh


def shares(nlon, nlat):
    px, nzl, nzh, py = groups(nlon, nlat)
    size = px * py * 2
    return size, nzl * nzh // 2, MAIN // size, max(16, (TOT - MAIN) // size)


def one_hot(shape, pick):
    a = lax.broadcasted_iota(jnp.int32, shape, 0)
    b = lax.broadcasted_iota(jnp.int32, shape, 1)
    return pick(a, b).astype(F32).astype(BF16)


def dot(a, b, contract=((1,), (0,))):
    return lax.dot_general(a, b, (contract, ((), ())), preferred_element_type=F32)


def remote(kind, src, dst, send, recv, target):
    return pltpu.make_async_remote_copy(
        src_ref=src,
        dst_ref=dst,
        send_sem=send,
        recv_sem=recv,
        device_id=target,
        device_id_type=MESH,
    )


def main_kernel(
    nlon,
    nlat,
    state_h,
    mask_h,
    cot_h,
    kern_h,
    gain_h,
    nbias_h,
    w_in_h,
    b_hid_h,
    w_out_h,
    b_out_h,
    scale_h,
    block_h,
    grad_h,
    total,
    block_out,
    grad_state,
    state,
    mask,
    cot,
    kern,
    gain,
    nbias,
    w_in,
    b_hid,
    w_out,
    b_out,
    scale,
    pad,
    shifted,
    padq,
    shiftq,
    taps,
    maskb,
    mixp,
    ghid_s,
    normed_s,
    precot_s,
    hidden_s,
    bcot_s,
    own_s,
    sums,
    sumh,
    small,
    csend,
    ksend,
    crecv,
    vrecv,
    wbuf,
    wrecv,
    psum,
    extra,
    pay,
    xrecv,
    payx,
    xrecvx,
    zslot,
    abuf,
    fin,
    load_s,
    store_s,
    halo_s,
    halo_r,
    core_s,
    core_r,
    xs,
    xr,
    xsx,
    xrx,
    zs,
    zr,
    xas,
    xar,
    ls,
    lr,
):
    px, nzl, nzh, py = groups(nlon, nlat)
    size, nz, mrows, erows = shares(nlon, nlat)

    loads = [
        pltpu.make_async_copy(src, dst, load_s.at[i])
        for i, (src, dst) in enumerate(
            (
                (state_h, state),
                (mask_h, mask),
                (kern_h, kern),
                (cot_h, cot),
                (w_in_h, w_in),
                (w_out_h, w_out),
                (gain_h, gain),
                (nbias_h, nbias),
                (b_hid_h, b_hid),
                (b_out_h, b_out),
                (scale_h, scale),
            )
        )
    ]
    for load in loads[:3]:
        load.start()

    lon = lax.axis_index("lon")
    lat = lax.axis_index("lat")
    core = lax.rem(lon, 2)
    x = lax.rem(lax.div(lon, 2), px)
    zl = lax.div(lon, 2 * px)
    zh = lax.rem(lat, nzh)
    y = lax.div(lat, nzh)
    odd = lax.rem(zl, 2)
    me = (y * px + x) * 2 + odd
    zi = zh * (nzl // 2) + lax.div(zl, 2)
    is_top = lat == nlat - 1
    has_south = lat > 0

    def device(la, lo):
        return {"lon": lo, "lat": la}

    right, left = lax.rem(lon + 1, nlon), lax.rem(lon + nlon - 1, nlon)
    above, below = jnp.where(is_top, lat, lat + 1), jnp.where(has_south, lat - 1, 0)
    fold_r, fold_l = lax.rem(2 * nlon - 2 - lon, nlon), lax.rem(nlon - lon, nlon)
    east, west = device(lat, right), device(lat, left)
    north = device(above, jnp.where(is_top, nlon - 1 - lon, lon))
    south = device(below, lon)
    top_r = device(above, jnp.where(is_top, fold_r, right))
    top_l = device(above, jnp.where(is_top, fold_l, left))
    bot_r, bot_l = device(below, right), device(below, left)
    self_r = jnp.logical_and(is_top, fold_r == lon)
    self_l = jnp.logical_and(is_top, fold_l == lon)
    other_r, other_l = jnp.logical_not(self_r), jnp.logical_not(self_l)
    pair = device(lat, lon + 1 - 2 * core)

    def in_group(k):
        p = lax.div(k, 2)
        z = zl - odd + lax.rem(k, 2)
        return device(lax.div(p, px) * nzh + zh, z * (2 * px) + lax.rem(p, px) * 2 + core)

    def in_z(k):
        z = lax.rem(k, nzl // 2) * 2 + odd
        return device(y * nzh + lax.div(k, nzl // 2), z * (2 * px) + x * 2 + core)

    def shift(field, out):
        @pl.loop(0, PADR)
        def _(r):
            for b in range(7):
                out[b, r] = field[r, 5 + b : 21 + b, :].reshape(2, 8, C)

    def inner(b, h):
        return b >= 3 if h == 0 else b <= 3

    def shift_some(r, wanted):
        for b in range(7):
            for h in range(2):
                if wanted(b, h):
                    shifted[b, r, h] = pad[r, 5 + b + 8 * h : 13 + b + 8 * h, :]

    def conv_half(r0, h, wanted, acc):
        for b in range(7):
            if wanted(b, h):
                win = shifted[b, pl.ds(r0, 10), h]
                for a in range(7):
                    acc = acc + win[a : a + 4] * taps[a * 7 + b]
        return acc

    def conv_inner(r0):
        for h in range(2):
            mixp[pl.ds(r0, 4), h] = conv_half(r0, h, inner, jnp.zeros((4, 8, C), F32))

    def conv_outer(r0):
        halves = [
            conv_half(r0, h, lambda b, h: not inner(b, h), mixp[pl.ds(r0, 4), h]) for h in range(2)
        ]
        return jnp.stack(halves, axis=1).reshape(4 * COLS, C)

    def conv_rows(source, r0, rows, flip):
        acc = jnp.zeros((rows, 2, 8, C), F32)
        for b in range(7):
            win = source[b, pl.ds(r0, rows + 6)]
            for a in range(7):
                k = taps[48 - a * 7 - b] if flip else taps[a * 7 + b]
                acc = acc + win[a : a + rows] * k
        return acc

    barrier = pltpu.get_barrier_semaphore()

    def hello(target):
        pl.semaphore_signal(barrier, inc=1, device_id=target, device_id_type=MESH)

    hello(north)

    @pl.when(has_south)
    def _():
        hello(south)
        hello(bot_r)
        hello(bot_l)

    @pl.when(other_r)
    def _():
        hello(top_r)

    @pl.when(other_l)
    def _():
        hello(top_l)

    hello(east)
    hello(west)

    @pl.loop(1, nz)
    def _(d):
        hello(in_z(lax.rem(zi + d, nz)))

    @pl.loop(1, size)
    def _(d):
        hello(in_group(lax.rem(me + d, size)))

    hello(pair)
    for load in loads[3:]:
        load.start()

    by_row = one_hot((CELLS, ROWS), lambda a, b: a // COLS == b)
    by_col = one_hot((CELLS, COLS), lambda a, b: a % COLS == b).astype(F32)

    def pick_cell(a):
        e = (a // 3) * COLS + 13 + a % 3
        w = ((a - 96) // 3) * COLS + (a - 96) % 3
        c, i = (a - 192) // 16, (a - 192) % 16
        corner = (i // 3 + (ROWS - 3) * (c // 2)) * COLS + i % 3 + 13 * (c % 2)
        return jnp.where(a < 96, e, jnp.where(a < 192, w, jnp.where(i < 9, corner, -1)))

    picks = one_hot((256, CELLS), lambda a, b: pick_cell(a) == b)
    left_put = one_hot(
        (ROWS * 8, 96), lambda a, b: (a % 8 >= 5) & ((a // 8) * 3 + a % 8 - 5 == b)
    )
    right_put = one_hot((ROWS * 8, 96), lambda a, b: (a % 8 < 3) & ((a // 8) * 3 + a % 8 == b))

    def put_cell(a, fold):
        m, q = a // WIDE, a % WIDE
        row = jnp.where(fold, 2 - m, m)
        mid = row * COLS + jnp.where(fold, 23 - q, q - 8)
        lo = 48 + row * 3 + jnp.where(fold, 7 - q, q - 5)
        hi = 64 + row * 3 + jnp.where(fold, 26 - q, q - 24)
        hi = jnp.where((q >= 24) & (q < 27), hi, -1)
        return jnp.where((q >= 8) & (q < 24), mid, jnp.where((q >= 5) & (q < 8), lo, hi))

    north_put = one_hot((3 * WIDE, 80), lambda a, b: put_cell(a, is_top) == b)
    south_put = one_hot((3 * WIDE, 80), lambda a, b: put_cell(a, False) == b)

    def halo_copies(n):
        slot = jnp.where(is_top, 0, 1)

        def copy(src, dst, s, r, target):
            return remote("halo", src, dst, halo_s.at[n, s], halo_r.at[n, r], target)

        corner = ksend.at[n]
        return dict(
            e=copy(csend.at[n, 0], crecv.at[n, 0], 0, 0, east),
            w=copy(csend.at[n, 1], crecv.at[n, 1], 1, 1, west),
            up=copy(own_s.at[n, ROWS - 3 : ROWS], vrecv.at[n, slot, 0:3], 2, 2 + slot, north),
            tr=copy(
                corner.at[3],
                vrecv.at[n, slot, 4 - slot],
                3,
                jnp.where(is_top, 5, 6),
                top_r,
            ),
            tl=copy(
                corner.at[2],
                vrecv.at[n, slot, 3 + slot],
                4,
                jnp.where(is_top, 4, 7),
                top_l,
            ),
            down=copy(own_s.at[n, 0:3], vrecv.at[n, 0, 0:3], 5, 2, south),
            br=copy(corner.at[1], vrecv.at[n, 0, 3], 6, 4, bot_r),
            bl=copy(corner.at[0], vrecv.at[n, 0, 4], 7, 5, bot_l),
        )

    def pick_halo(n):
        picked = dot(picks, own_s[n].reshape(CELLS, C)).astype(BF16)
        csend[n] = picked[0:192].reshape(2, 96, C)
        ksend[n] = picked[192:256].reshape(4, 16, C)

    def send_halo(n):
        copies = halo_copies(n)
        copies["up"].start()

        @pl.when(has_south)
        def _():
            copies["down"].start()
            copies["br"].start()
            copies["bl"].start()

        @pl.when(other_r)
        def _():
            copies["tr"].start()

        @pl.when(other_l)
        def _():
            copies["tl"].start()

        copies["e"].start()
        copies["w"].start()

        @pl.when(self_r)
        def _():
            vrecv[n, 0, 4] = ksend[n, 3]

        @pl.when(self_l)
        def _():
            vrecv[n, 0, 3] = ksend[n, 2]

    def take_halo(n, field):
        copies = halo_copies(n)

        def arrive(piece, r):
            remote("halo", piece, piece, halo_s.at[n, 0], halo_r.at[n, r], east).wait_recv()

        copies["e"].wait()
        copies["w"].wait()
        field[3 : 3 + ROWS, 0:8, :] = dot(left_put, crecv[n, 0]).reshape(ROWS, 8, C)
        field[3 : 3 + ROWS, 24:32, :] = dot(right_put, crecv[n, 1]).reshape(ROWS, 8, C)
        copies["up"].wait_send()
        arrive(vrecv.at[n, 0, 0:3], 2)

        @pl.when(other_r)
        def _():
            copies["tr"].wait_send()
            arrive(vrecv.at[n, 0, 4], 5)

        @pl.when(other_l)
        def _():
            copies["tl"].wait_send()
            arrive(vrecv.at[n, 0, 3], 4)

        field[ROWS + 3 : ROWS + 6] = dot(north_put, vrecv[n, 0].reshape(80, C)).reshape(3, WIDE, C)

        @pl.when(has_south)
        def _():
            for name in ("down", "br", "bl"):
                copies[name].wait_send()
            arrive(vrecv.at[n, 1, 0:3], 3)
            arrive(vrecv.at[n, 1, 3], 6)
            arrive(vrecv.at[n, 1, 4], 7)
            field[0:3] = dot(south_put, vrecv[n, 1].reshape(80, C)).reshape(3, WIDE, C)

        @pl.when(jnp.logical_not(has_south))
        def _():
            field[0:3] = jnp.zeros((3, WIDE, C), F32)

    for load in loads[:3]:
        load.wait()
    sea = dot(by_row, mask[...].astype(F32).astype(BF16), ((1,), (1,))) * by_col
    maskb[...] = dot(sea.astype(BF16), jnp.ones((COLS, C), BF16)).reshape(ROWS, COLS, C)
    own = state[...].astype(F32) * maskb[...]
    pad[3 : 3 + ROWS, 8:24, :] = own
    own_s[0] = own.astype(BF16)
    pick_halo(0)
    for a in range(7):
        k7 = kern[a].astype(F32)
        for b in range(7):
            taps[a * 7 + b] = jnp.broadcast_to(k7[b : b + 1], (8, C))
    sums[...] = jnp.zeros_like(sums)
    sumh[...] = jnp.zeros_like(sumh)
    small[...] = jnp.zeros_like(small)
    extra[...] = jnp.zeros_like(extra)

    hellos = 4 + (size - 1) + (nz - 1) + jnp.where(has_south, 3, 0)
    hellos = hellos + jnp.where(other_r, 1, 0) + jnp.where(other_l, 1, 0)
    pl.semaphore_wait(barrier, hellos)
    send_halo(0)
    for load in loads[3:]:
        load.wait()

    ct_all = cot[...].astype(F32) * maskb[...]
    gb_all = (ct_all * scale[...].reshape(1, 1, C)).reshape(CELLS, C)
    bcot_s[...] = gb_all.astype(BF16)
    sums[2] = jnp.sum(gb_all.reshape(CELLS // 8, 8, C), axis=0)
    for t in range(HID // 256):
        wide = slice(256 * t, 256 * t + 256)
        ghid_s[:, wide] = dot(bcot_s[...], w_out[:, wide])

    @pl.loop(3, 3 + ROWS, unroll=4)
    def _(r):
        shift_some(r, inner)

    @pl.loop(1, ROWS // 4 - 1)
    def _(i):
        conv_inner(4 * i)

    take_halo(0, pad)

    @pl.loop(3, 3 + ROWS, unroll=4)
    def _(r):
        shift_some(r, lambda b, h: not inner(b, h))

    for q in range(3):
        shift_some(q, lambda b, h: True)
        shift_some(ROWS + 3 + q, lambda b, h: True)
    conv_inner(0)
    conv_inner(ROWS - 4)

    block = ROWS
    cells = block * COLS

    @pl.loop(0, ROWS // block)
    def _(blk):
        r0 = blk * block
        here = pl.ds(pl.multiple_of(r0 * COLS, cells), cells)
        mixed = jnp.concatenate(
            [conv_outer(r0 + 4 * i) for i in range(block // 4)],
            axis=0,
        )
        average = jnp.sum(mixed, axis=1, keepdims=True) * (1.0 / C)
        centred = mixed - average
        variance = jnp.sum(centred * centred, axis=1, keepdims=True) * (1.0 / C)
        inv_std = lax.rsqrt(variance + EPSILON)
        unit = centred * inv_std
        normed = (unit * gain[...] + nbias[...]).astype(BF16)
        normed_s[here, :] = normed
        pre = dot(normed, w_in[...]) + b_hid[...].reshape(HID)
        square = pre * pre
        t = jnp.tanh(GELU_A * pre * (1.0 + GELU_B * square))
        half = 0.5 * (1.0 + t)
        hidden = (pre * half).astype(BF16)
        hidden_s[here, :] = hidden
        slope = half + pre * (0.5 * GELU_A) * (1.0 - t * t) * (1.0 + 3.0 * GELU_B * square)
        branch = dot(hidden, w_out[...], ((1,), (1,))) + b_out[...]
        rows_here = pl.ds(r0, block)
        sea_w = maskb[rows_here].reshape(cells, C)
        st = state[rows_here].astype(F32).reshape(cells, C)
        ct = cot[rows_here].astype(F32).reshape(cells, C) * sea_w
        block_out[rows_here] = (
            (sea_w * (st + scale[...] * branch)).astype(BF16).reshape(block, COLS, C)
        )
        grad_pre = ghid_s[here, :] * slope
        precot = grad_pre.astype(BF16)
        precot_s[here, :] = precot
        grad_normed = dot(precot, w_in[...], ((1,), (1,)))
        grad_unit = grad_normed * gain[...]
        mean_a = jnp.sum(grad_unit, axis=1, keepdims=True) * (1.0 / C)
        mean_b = jnp.sum(grad_unit * unit, axis=1, keepdims=True) * (1.0 / C)
        grad_mixed = inv_std * (grad_unit - mean_a - unit * mean_b)
        mcot = grad_mixed.astype(BF16)
        own_s[1, rows_here] = mcot.reshape(block, COLS, C)
        padq[pl.ds(3 + r0, block), 8:24, :] = mcot.astype(F32).reshape(block, COLS, C)

        def fold8(v):
            return jnp.sum(v.reshape(cells // 8, 8, v.shape[1]), axis=0)

        sums[0] += fold8(grad_normed * unit)
        sums[1] += fold8(grad_normed)
        sums[3] += fold8(ct * branch)
        sumh[...] += fold8(grad_pre)

    pick_halo(1)
    block_store = pltpu.make_async_copy(block_out, block_h, store_s.at[0])
    block_store.start()

    for t in range(HID // 256):
        wide = slice(256 * t, 256 * t + 256)
        g_in = dot(normed_s[...], precot_s[:, wide], ((0,), (0,)))
        g_out = dot(bcot_s[...], hidden_s[:, wide], ((0,), (0,)))
        for j in range(2):
            to = slice((2 * t + j) * C, (2 * t + j + 1) * C)
            wbuf[0, to, :] = g_in[:, 128 * j : 128 * j + 128]
            wbuf[1, to, :] = g_out[:, 128 * j : 128 * j + 128]

    def to_pair(i, rows):
        return remote("pair", wbuf.at[1 - core, rows], wrecv.at[rows], core_s.at[i], core_r.at[i], pair)

    pair_w = to_pair(0, pl.ds(0, WROWS))
    pair_w.start()

    def kernel_grad(b):
        def step(i, accs):
            r0 = i * 4
            m = padq[pl.ds(3 + r0, 4), 8:24, :].reshape(4, 2, 8, C)
            win = shifted[b, pl.ds(r0, 10)]
            return tuple(
                accs[a] + jnp.sum((m * win[a : a + 4]).reshape(8, 8, C), axis=0)
                for a in range(7)
            )

        accs = lax.fori_loop(0, ROWS // 4, step, tuple(jnp.zeros((8, C), F32) for _ in range(7)))
        for a in range(7):
            small[a * 7 + b : a * 7 + b + 1, 0:C] = jnp.sum(accs[a], axis=0, keepdims=True)

    for b in range(3):
        kernel_grad(b)

    def group_copy(k, sender):
        return remote("group", pay.at[k], xrecv.at[sender], xs.at[k], xr.at[sender], in_group(k))

    def rest_copy(k, sender):
        return remote("group", payx.at[k], xrecvx.at[sender], xsx.at[k], xrx.at[sender], in_group(k))

    pair_w.wait()

    def add_pair(k):
        rows = pl.ds(pl.multiple_of(k * mrows, 32), mrows)
        both = wbuf[core, rows, :] + wrecv[rows, :]
        psum[rows, :] = both
        pay[k] = both.astype(BF16)

    add_pair(me)

    def far(i, n, first):
        return 1 + lax.rem(i + first, n - 1)

    @pl.loop(0, size - 1)
    def _(i):
        k = lax.rem(me + far(i, size, size * 5 // 8 - 1), size)
        add_pair(k)
        group_copy(k, me).start()

    send_halo(1)

    for b in range(3, 7):
        kernel_grad(b)
    for i in range(4):
        small[49 + i : 50 + i, 0:C] = jnp.sum(sums[i], axis=0, keepdims=True)
    hid_row = jnp.sum(sumh[...], axis=0, keepdims=True)
    for i in range(3):
        small[53 + i : 54 + i, :] = hid_row[:, 256 * i : 256 * i + 256]
    wbuf[0, WROWS:, :] = small[:, 0:128]
    wbuf[1, WROWS:, :] = small[:, 128:256]
    pair_s = to_pair(1, pl.ds(WROWS, SROWS))
    pair_s.start()

    pair_s.wait()
    rest_w = wbuf[core, MAIN:WROWS, :] + wrecv[MAIN:WROWS, :]
    both = wbuf[core, WROWS:, :] + wrecv[WROWS:, :]
    high = both.astype(BF16).astype(F32)
    other = jnp.concatenate([rest_w, high, both - high], axis=0)
    for i in range((TOT - MAIN) // size):
        extra[pl.ds(i, size, stride=erows), :] = other[i * size : (i + 1) * size]
    payx[...] = extra[...].reshape(size, erows, 128).astype(BF16)

    @pl.loop(0, size - 1)
    def _(i):
        k = lax.rem(me + far(i, size, size * 5 // 8 - 1), size)
        rest_copy(k, me).start()

    def halves(v):
        first = (WROWS - MAIN) // size
        count = SROWS // size
        end = v.shape[0]
        row = lax.broadcasted_iota(jnp.int32, v.shape, 0) - mrows
        whole = v + pltpu.roll(v, end - count, 0)
        top = whole.astype(BF16).astype(F32)
        low = pltpu.roll(whole - top, count, 0)
        is_high = (row >= first) & (row < first + count)
        is_low = (row >= first + count) & (row < first + 2 * count)
        return jnp.where(is_high, top, jnp.where(is_low, low, v)).astype(BF16)

    @pl.loop(1, size)
    def _(d):
        k = lax.rem(me + d, size)
        group_copy(k, k).wait()

    def add_main(d, acc):
        return acc + xrecv[lax.rem(me + d, size)].astype(F32)

    def add_rest(d, acc):
        return acc + xrecvx[lax.rem(me + d, size)].astype(F32)

    mine = psum[pl.ds(pl.multiple_of(me * mrows, 32), mrows), :]
    mine = lax.fori_loop(1, size, add_main, mine)

    @pl.loop(1, size)
    def _(d):
        k = lax.rem(me + d, size)
        rest_copy(k, k).wait()

    minex = extra[pl.ds(pl.multiple_of(me * erows, 16), erows), :]
    minex = lax.fori_loop(1, size, add_rest, minex)
    zslot[zi] = halves(jnp.concatenate([mine, minex], axis=0))

    def z_copy(k, sender):
        return remote("z", zslot.at[sender], zslot.at[sender], zs.at[k], zr.at[sender], in_z(k))

    @pl.loop(0, nz - 1)
    def _(i):
        z_copy(lax.rem(zi + far(i, nz, nz // 2 - 1), nz), zi).start()

    take_halo(1, padq)
    shift(padq, shiftq)

    @pl.loop(0, ROWS // 2)
    def _(i):
        rows_here = pl.ds(i * 2, 2)
        grad = conv_rows(shiftq, i * 2, 2, True).reshape(2, COLS, C)
        grad_state[rows_here] = (
            maskb[rows_here] * (cot[rows_here].astype(F32) + grad)
        ).astype(BF16)

    @pl.when(is_top)
    def _():
        first = ROWS - 4
        acc = conv_rows(shiftq, first, 4, True)
        parts = [acc[i] for i in range(4)]
        for i in range(1, 4):
            for a in range(7 - i, 7):
                for b in range(7):
                    change = taps[a * 7 + b] - taps[48 - a * 7 - b]
                    parts[i] = parts[i] + shiftq[b, first + i + a] * change
        for i in range(1, 4):
            grad_state[first + i] = (
                maskb[first + i] * (cot[first + i].astype(F32) + parts[i].reshape(COLS, C))
            ).astype(BF16)

    grad_store = pltpu.make_async_copy(grad_state, grad_h, store_s.at[1])
    grad_store.start()

    @pl.loop(1, nz)
    def _(d):
        k = lax.rem(zi + d, nz)
        z_copy(k, k).wait()

    whole = zslot[0].astype(F32)
    for k in range(1, nz):
        whole = whole + zslot[k].astype(F32)
    abuf[me] = halves(whole)

    def back_copy(owner, k):
        return remote("back", abuf.at[owner], abuf.at[owner], xas.at[k], xar.at[owner], in_group(k))

    @pl.loop(0, size - 1)
    def _(i):
        back_copy(me, lax.rem(me + far(i, size, size * 5 // 8 - 1), size)).start()

    def last_copy(k):
        return remote("last", abuf.at[k], fin.at[k], ls.at[k], lr.at[k], pair)

    last_copy(me).start()

    @pl.loop(1, size)
    def _(d):
        k = lax.rem(me + d, size)
        back_copy(k, k).wait()
        last_copy(k).start()

    own_store = pltpu.make_async_copy(abuf, total.at[core], store_s.at[2])
    own_store.start()

    @pl.loop(0, size)
    def _(k):
        last_copy(k).wait()

    fin_store = pltpu.make_async_copy(fin, total.at[1 - core], store_s.at[3])
    fin_store.start()
    for store in (block_store, grad_store, own_store, fin_store):
        store.wait()


def finish_kernel(
    factor, size, mrows, erows, total_h, block_h, grad_h,
    block_out, grad_out, gk, gg, gb, gw_in, gbh, gw_out, gbo, gls, total, extra, sem,
):
    moves = [
        pltpu.make_async_copy(src, dst, sem.at[i])
        for i, (src, dst) in enumerate(
            ((total_h, total), (block_h, block_out), (grad_h, grad_out))
        )
    ]
    for move in moves:
        move.start()
    moves[0].wait()
    small = []
    for c, gw in ((0, gw_in), (1, gw_out)):
        rows = total[c, :, 0:mrows, :].reshape(MAIN, 128).astype(F32) * factor
        extra[...] = total[c, :, mrows:, :].reshape(size * erows, 128).astype(F32) * factor
        rest = [extra[pl.ds(i, size, stride=erows), :] for i in range((TOT - MAIN) // size)]
        rows = jnp.concatenate([rows] + rest, axis=0)
        for t in range(HID // 128):
            gw[:, 128 * t : 128 * t + 128] = rows[t * C : (t + 1) * C]
        small.append(rows[WROWS : WROWS + SROWS] + rows[WROWS + SROWS :])
    near, far = small
    for a in range(7):
        gk[a, :, 0:128] = near[7 * a : 7 * a + 7]
        gk[a, :, 128:C] = far[7 * a : 7 * a + 7, 0 : C - 128]
    for i, out in enumerate((gg, gb, gbo, gls)):
        out[:, 0:128] = near[49 + i : 50 + i]
        out[:, 128:C] = far[49 + i : 50 + i, 0 : C - 128]
    for i in range(3):
        gbh[256 * i : 256 * i + 128] = near[53 + i]
        gbh[256 * i + 128 : 256 * i + 256] = far[53 + i]
    for move in moves[1:]:
        move.wait()


def on_device(
    nlon,
    nlat,
    state,
    land_mask,
    cotangent,
    kernel,
    norm_gain,
    norm_bias,
    weight_in,
    bias_hidden,
    weight_out,
    bias_out,
    layer_scale,
):
    size, nz, mrows, erows = shares(nlon, nlat)
    hbm = pl.BlockSpec(memory_space=pltpu.HBM)
    vmem = pl.BlockSpec(memory_space=pltpu.VMEM)
    dma = pltpu.SemaphoreType.DMA
    row = lambda v: v.reshape(1, -1)
    block, grad, total = pl.pallas_call(
        functools.partial(main_kernel, nlon, nlat),
        out_shape=(
            jax.ShapeDtypeStruct((ROWS, COLS, C), BF16),
            jax.ShapeDtypeStruct((ROWS, COLS, C), BF16),
            jax.ShapeDtypeStruct((2, size, mrows + erows, 128), BF16),
        ),
        in_specs=[hbm] * 11,
        out_specs=(hbm,) * 3,
        scratch_shapes=[
            pltpu.VMEM((ROWS, COLS, C), BF16),
            pltpu.VMEM((ROWS, COLS, C), BF16),
            pltpu.VMEM((ROWS, COLS, C), BF16),
            pltpu.VMEM((COLS, ROWS), jnp.int32),
            pltpu.VMEM((ROWS, COLS, C), BF16),
            pltpu.VMEM((7, 7, C), BF16),
            pltpu.VMEM((1, C), F32),
            pltpu.VMEM((1, C), F32),
            pltpu.VMEM((C, HID), BF16),
            pltpu.VMEM((HID,), F32),
            pltpu.VMEM((C, HID), BF16),
            pltpu.VMEM((1, C), F32),
            pltpu.VMEM((1, C), F32),
            pltpu.VMEM((PADR, WIDE, C), F32),
            pltpu.VMEM((7, PADR, 2, 8, C), F32),
            pltpu.VMEM((PADR, WIDE, C), F32),
            pltpu.VMEM((7, PADR, 2, 8, C), F32),
            pltpu.VMEM((49, 8, C), F32),
            pltpu.VMEM((ROWS, COLS, C), F32),
            pltpu.VMEM((ROWS, 2, 8, C), F32),
            pltpu.VMEM((CELLS, HID), F32),
            pltpu.VMEM((CELLS, C), BF16),
            pltpu.VMEM((CELLS, HID), BF16),
            pltpu.VMEM((CELLS, HID), BF16),
            pltpu.VMEM((CELLS, C), BF16),
            pltpu.VMEM((2, ROWS, COLS, C), BF16),
            pltpu.VMEM((4, 8, C), F32),
            pltpu.VMEM((8, HID), F32),
            pltpu.VMEM((SROWS, 256), F32),
            pltpu.VMEM((2, 2, 96, C), BF16),
            pltpu.VMEM((2, 4, 16, C), BF16),
            pltpu.VMEM((2, 2, 96, C), BF16),
            pltpu.VMEM((2, 2, 5, 16, C), BF16),
            pltpu.VMEM((2, WROWS + SROWS, 128), F32),
            pltpu.VMEM((WROWS + SROWS, 128), F32),
            pltpu.VMEM((MAIN, 128), F32),
            pltpu.VMEM((size * erows, 128), F32),
            pltpu.VMEM((size, mrows, 128), BF16),
            pltpu.VMEM((size, mrows, 128), BF16),
            pltpu.VMEM((size, erows, 128), BF16),
            pltpu.VMEM((size, erows, 128), BF16),
            pltpu.VMEM((nz, mrows + erows, 128), BF16),
            pltpu.VMEM((size, mrows + erows, 128), BF16),
            pltpu.VMEM((size, mrows + erows, 128), BF16),
            dma((11,)),
            dma((4,)),
            dma((2, 8)),
            dma((2, 8)),
            dma((2,)),
            dma((2,)),
            dma((size,)),
            dma((size,)),
            dma((size,)),
            dma((size,)),
            dma((nz,)),
            dma((nz,)),
            dma((size,)),
            dma((size,)),
            dma((size,)),
            dma((size,)),
        ],
        compiler_params=pltpu.CompilerParams(
            collective_id=0, has_side_effects=True, vmem_limit_bytes=56 * 1024 * 1024
        ),
        name="block",
    )(
        state,
        land_mask.T,
        cotangent,
        kernel,
        row(norm_gain),
        row(norm_bias),
        weight_in,
        bias_hidden,
        weight_out.T,
        row(bias_out),
        row(layer_scale),
    )
    factor = 1.0 / math.sqrt(ROWS * nlat * COLS * nlon)
    shape = lambda *s: jax.ShapeDtypeStruct(s, F32)
    outs = pl.pallas_call(
        functools.partial(finish_kernel, factor, size, mrows, erows),
        out_shape=(
            jax.ShapeDtypeStruct((ROWS, COLS, C), BF16),
            jax.ShapeDtypeStruct((ROWS, COLS, C), BF16),
            shape(7, 7, C),
            shape(1, C),
            shape(1, C),
            shape(C, HID),
            shape(HID),
            shape(C, HID),
            shape(1, C),
            shape(1, C),
        ),
        in_specs=[hbm] * 3,
        out_specs=(vmem,) * 10,
        scratch_shapes=[
            pltpu.VMEM((2, size, mrows + erows, 128), BF16),
            pltpu.VMEM((size * erows, 128), F32),
            dma((3,)),
        ],
        compiler_params=pltpu.CompilerParams(vmem_limit_bytes=56 * 1024 * 1024),
        name="finish",
    )(total, block, grad)
    outs = [o.reshape(-1) if o.shape[0] == 1 else o for o in outs]
    outs[7] = outs[7].T
    return tuple(outs)


def solution(mesh):
    cells, plane, whole = P("lat", "lon", None), P("lat", "lon"), P()
    return jax.shard_map(
        functools.partial(on_device, mesh.shape["lon"], mesh.shape["lat"]),
        mesh=mesh,
        in_specs=(cells, plane, cells) + (whole,) * 8,
        out_specs=(cells, cells) + (whole,) * 8,
        check_vma=False,
    )
```

```python
import functools
import math

import jax
import jax.numpy as jnp
from jax import lax
from jax.experimental import pallas as pl
from jax.experimental.pallas import tpu as pltpu
from jax.sharding import PartitionSpec as P

EPSILON = 1e-06
MESH = pl.DeviceIdType.MESH
F32 = jnp.float32
BF16 = jnp.bfloat16

ROWS, COLS, C, HID = 32, 16, 192, 768
CELLS = ROWS * COLS
PADR, WIDE = ROWS + 6, 32
WROWS = C * HID // 128
SROWS = 64
TOT = WROWS + 2 * SROWS
MAIN = 1024
GELU_A = math.sqrt(2.0 / math.pi)
GELU_B = 0.044715


def groups(nlon, nlat):
    px = 4 if nlon >= 64 else 1
    nzl = nlon // (2 * px)
    nzh = 2 if nlat >= 8 else 1
    return px, nzl, nzh, nlat // nzh


def shares(nlon, nlat):
    px, nzl, nzh, py = groups(nlon, nlat)
    size = px * py * 2
    return size, nzl * nzh // 2, MAIN // size, max(16, (TOT - MAIN) // size)


def one_hot(shape, pick):
    a = lax.broadcasted_iota(jnp.int32, shape, 0)
    b = lax.broadcasted_iota(jnp.int32, shape, 1)
    return pick(a, b).astype(F32).astype(BF16)


def dot(a, b, contract=((1,), (0,))):
    return lax.dot_general(a, b, (contract, ((), ())), preferred_element_type=F32)


def remote(kind, src, dst, send, recv, target):
    return pltpu.make_async_remote_copy(
        src_ref=src,
        dst_ref=dst,
        send_sem=send,
        recv_sem=recv,
        device_id=target,
        device_id_type=MESH,
    )


def main_kernel(
    nlon,
    nlat,
    state_h,
    mask_h,
    cot_h,
    kern_h,
    gain_h,
    nbias_h,
    w_in_h,
    b_hid_h,
    w_out_h,
    b_out_h,
    scale_h,
    block_h,
    grad_h,
    total,
    block_out,
    grad_state,
    state,
    mask,
    cot,
    kern,
    gain,
    nbias,
    w_in,
    b_hid,
    w_out,
    b_out,
    scale,
    pad,
    shifted,
    padq,
    shiftq,
    taps,
    maskb,
    mixp,
    ghid_s,
    normed_s,
    precot_s,
    hidden_s,
    bcot_s,
    own_s,
    sums,
    sumh,
    small,
    csend,
    ksend,
    crecv,
    vrecv,
    wbuf,
    wrecv,
    psum,
    extra,
    pay,
    xrecv,
    payx,
    xrecvx,
    zslot,
    abuf,
    fin,
    load_s,
    store_s,
    halo_s,
    halo_r,
    core_s,
    core_r,
    xs,
    xr,
    xsx,
    xrx,
    zs,
    zr,
    xas,
    xar,
    ls,
    lr,
):
    px, nzl, nzh, py = groups(nlon, nlat)
    size, nz, mrows, erows = shares(nlon, nlat)

    loads = [
        pltpu.make_async_copy(src, dst, load_s.at[i])
        for i, (src, dst) in enumerate(
            (
                (state_h, state),
                (mask_h, mask),
                (kern_h, kern),
                (cot_h, cot),
                (w_in_h, w_in),
                (w_out_h, w_out),
                (gain_h, gain),
                (nbias_h, nbias),
                (b_hid_h, b_hid),
                (b_out_h, b_out),
                (scale_h, scale),
            )
        )
    ]
    for load in loads[:3]:
        load.start()

    lon = lax.axis_index("lon")
    lat = lax.axis_index("lat")
    core = lax.rem(lon, 2)
    x = lax.rem(lax.div(lon, 2), px)
    zl = lax.div(lon, 2 * px)
    zh = lax.rem(lat, nzh)
    y = lax.div(lat, nzh)
    odd = lax.rem(zl, 2)
    me = (y * px + x) * 2 + odd
    zi = zh * (nzl // 2) + lax.div(zl, 2)
    is_top = lat == nlat - 1
    has_south = lat > 0

    def device(la, lo):
        return {"lon": lo, "lat": la}

    right, left = lax.rem(lon + 1, nlon), lax.rem(lon + nlon - 1, nlon)
    above, below = jnp.where(is_top, lat, lat + 1), jnp.where(has_south, lat - 1, 0)
    fold_r, fold_l = lax.rem(2 * nlon - 2 - lon, nlon), lax.rem(nlon - lon, nlon)
    east, west = device(lat, right), device(lat, left)
    north = device(above, jnp.where(is_top, nlon - 1 - lon, lon))
    south = device(below, lon)
    top_r = device(above, jnp.where(is_top, fold_r, right))
    top_l = device(above, jnp.where(is_top, fold_l, left))
    bot_r, bot_l = device(below, right), device(below, left)
    self_r = jnp.logical_and(is_top, fold_r == lon)
    self_l = jnp.logical_and(is_top, fold_l == lon)
    other_r, other_l = jnp.logical_not(self_r), jnp.logical_not(self_l)
    pair = device(lat, lon + 1 - 2 * core)

    def in_group(k):
        p = lax.div(k, 2)
        z = zl - odd + lax.rem(k, 2)
        return device(lax.div(p, px) * nzh + zh, z * (2 * px) + lax.rem(p, px) * 2 + core)

    def in_z(k):
        z = lax.rem(k, nzl // 2) * 2 + odd
        return device(y * nzh + lax.div(k, nzl // 2), z * (2 * px) + x * 2 + core)

    def shift(field, out):
        @pl.loop(0, PADR)
        def _(r):
            for b in range(7):
                out[b, r] = field[r, 5 + b : 21 + b, :].reshape(2, 8, C)

    def inner(b, h):
        return b >= 3 if h == 0 else b <= 3

    def shift_some(r, wanted):
        for b in range(7):
            for h in range(2):
                if wanted(b, h):
                    shifted[b, r, h] = pad[r, 5 + b + 8 * h : 13 + b + 8 * h, :]

    def conv_half(r0, h, wanted, acc):
        for b in range(7):
            if wanted(b, h):
                win = shifted[b, pl.ds(r0, 10), h]
                for a in range(7):
                    acc = acc + win[a : a + 4] * taps[a * 7 + b]
        return acc

    def conv_inner(r0):
        for h in range(2):
            mixp[pl.ds(r0, 4), h] = conv_half(r0, h, inner, jnp.zeros((4, 8, C), F32))

    def conv_outer(r0):
        halves = [
            conv_half(r0, h, lambda b, h: not inner(b, h), mixp[pl.ds(r0, 4), h]) for h in range(2)
        ]
        return jnp.stack(halves, axis=1).reshape(4 * COLS, C)

    def conv_rows(source, r0, rows, flip):
        acc = jnp.zeros((rows, 2, 8, C), F32)
        for b in range(7):
            win = source[b, pl.ds(r0, rows + 6)]
            for a in range(7):
                k = taps[48 - a * 7 - b] if flip else taps[a * 7 + b]
                acc = acc + win[a : a + rows] * k
        return acc

    barrier = pltpu.get_barrier_semaphore()

    def hello(target):
        pl.semaphore_signal(barrier, inc=1, device_id=target, device_id_type=MESH)

    hello(north)

    @pl.when(has_south)
    def _():
        hello(south)
        hello(bot_r)
        hello(bot_l)

    @pl.when(other_r)
    def _():
        hello(top_r)

    @pl.when(other_l)
    def _():
        hello(top_l)

    hello(east)
    hello(west)

    @pl.loop(1, nz)
    def _(d):
        hello(in_z(lax.rem(zi + d, nz)))

    @pl.loop(1, size)
    def _(d):
        hello(in_group(lax.rem(me + d, size)))

    hello(pair)
    for load in loads[3:]:
        load.start()

    by_row = one_hot((CELLS, ROWS), lambda a, b: a // COLS == b)
    by_col = one_hot((CELLS, COLS), lambda a, b: a % COLS == b).astype(F32)

    def pick_cell(a):
        e = (a // 3) * COLS + 13 + a % 3
        w = ((a - 96) // 3) * COLS + (a - 96) % 3
        c, i = (a - 192) // 16, (a - 192) % 16
        corner = (i // 3 + (ROWS - 3) * (c // 2)) * COLS + i % 3 + 13 * (c % 2)
        return jnp.where(a < 96, e, jnp.where(a < 192, w, jnp.where(i < 9, corner, -1)))

    picks = one_hot((256, CELLS), lambda a, b: pick_cell(a) == b)
    left_put = one_hot(
        (ROWS * 8, 96), lambda a, b: (a % 8 >= 5) & ((a // 8) * 3 + a % 8 - 5 == b)
    )
    right_put = one_hot((ROWS * 8, 96), lambda a, b: (a % 8 < 3) & ((a // 8) * 3 + a % 8 == b))

    def put_cell(a, fold):
        m, q = a // WIDE, a % WIDE
        row = jnp.where(fold, 2 - m, m)
        mid = row * COLS + jnp.where(fold, 23 - q, q - 8)
        lo = 48 + row * 3 + jnp.where(fold, 7 - q, q - 5)
        hi = 64 + row * 3 + jnp.where(fold, 26 - q, q - 24)
        hi = jnp.where((q >= 24) & (q < 27), hi, -1)
        return jnp.where((q >= 8) & (q < 24), mid, jnp.where((q >= 5) & (q < 8), lo, hi))

    north_put = one_hot((3 * WIDE, 80), lambda a, b: put_cell(a, is_top) == b)
    south_put = one_hot((3 * WIDE, 80), lambda a, b: put_cell(a, False) == b)

    def halo_copies(n):
        slot = jnp.where(is_top, 0, 1)

        def copy(src, dst, s, r, target):
            return remote("halo", src, dst, halo_s.at[n, s], halo_r.at[n, r], target)

        corner = ksend.at[n]
        return dict(
            e=copy(csend.at[n, 0], crecv.at[n, 0], 0, 0, east),
            w=copy(csend.at[n, 1], crecv.at[n, 1], 1, 1, west),
            up=copy(own_s.at[n, ROWS - 3 : ROWS], vrecv.at[n, slot, 0:3], 2, 2 + slot, north),
            tr=copy(
                corner.at[3],
                vrecv.at[n, slot, 4 - slot],
                3,
                jnp.where(is_top, 5, 6),
                top_r,
            ),
            tl=copy(
                corner.at[2],
                vrecv.at[n, slot, 3 + slot],
                4,
                jnp.where(is_top, 4, 7),
                top_l,
            ),
            down=copy(own_s.at[n, 0:3], vrecv.at[n, 0, 0:3], 5, 2, south),
            br=copy(corner.at[1], vrecv.at[n, 0, 3], 6, 4, bot_r),
            bl=copy(corner.at[0], vrecv.at[n, 0, 4], 7, 5, bot_l),
        )

    def pick_halo(n):
        picked = dot(picks, own_s[n].reshape(CELLS, C)).astype(BF16)
        csend[n] = picked[0:192].reshape(2, 96, C)
        ksend[n] = picked[192:256].reshape(4, 16, C)

    def send_halo(n):
        copies = halo_copies(n)
        copies["up"].start()

        @pl.when(has_south)
        def _():
            copies["down"].start()
            copies["br"].start()
            copies["bl"].start()

        @pl.when(other_r)
        def _():
            copies["tr"].start()

        @pl.when(other_l)
        def _():
            copies["tl"].start()

        copies["e"].start()
        copies["w"].start()

        @pl.when(self_r)
        def _():
            vrecv[n, 0, 4] = ksend[n, 3]

        @pl.when(self_l)
        def _():
            vrecv[n, 0, 3] = ksend[n, 2]

    def take_halo(n, field):
        copies = halo_copies(n)

        def arrive(piece, r):
            remote("halo", piece, piece, halo_s.at[n, 0], halo_r.at[n, r], east).wait_recv()

        copies["e"].wait()
        copies["w"].wait()
        field[3 : 3 + ROWS, 0:8, :] = dot(left_put, crecv[n, 0]).reshape(ROWS, 8, C)
        field[3 : 3 + ROWS, 24:32, :] = dot(right_put, crecv[n, 1]).reshape(ROWS, 8, C)
        copies["up"].wait_send()
        arrive(vrecv.at[n, 0, 0:3], 2)

        @pl.when(other_r)
        def _():
            copies["tr"].wait_send()
            arrive(vrecv.at[n, 0, 4], 5)

        @pl.when(other_l)
        def _():
            copies["tl"].wait_send()
            arrive(vrecv.at[n, 0, 3], 4)

        field[ROWS + 3 : ROWS + 6] = dot(north_put, vrecv[n, 0].reshape(80, C)).reshape(3, WIDE, C)

        @pl.when(has_south)
        def _():
            for name in ("down", "br", "bl"):
                copies[name].wait_send()
            arrive(vrecv.at[n, 1, 0:3], 3)
            arrive(vrecv.at[n, 1, 3], 6)
            arrive(vrecv.at[n, 1, 4], 7)
            field[0:3] = dot(south_put, vrecv[n, 1].reshape(80, C)).reshape(3, WIDE, C)

        @pl.when(jnp.logical_not(has_south))
        def _():
            field[0:3] = jnp.zeros((3, WIDE, C), F32)

    for load in loads[:3]:
        load.wait()
    sea = dot(by_row, mask[...].astype(F32).astype(BF16), ((1,), (1,))) * by_col
    maskb[...] = dot(sea.astype(BF16), jnp.ones((COLS, C), BF16)).reshape(ROWS, COLS, C)
    own = state[...].astype(F32) * maskb[...]
    pad[3 : 3 + ROWS, 8:24, :] = own
    own_s[0] = own.astype(BF16)
    pick_halo(0)
    for a in range(7):
        k7 = kern[a].astype(F32)
        for b in range(7):
            taps[a * 7 + b] = jnp.broadcast_to(k7[b : b + 1], (8, C))
    sums[...] = jnp.zeros_like(sums)
    sumh[...] = jnp.zeros_like(sumh)
    small[...] = jnp.zeros_like(small)
    extra[...] = jnp.zeros_like(extra)

    hellos = 4 + (size - 1) + (nz - 1) + jnp.where(has_south, 3, 0)
    hellos = hellos + jnp.where(other_r, 1, 0) + jnp.where(other_l, 1, 0)
    pl.semaphore_wait(barrier, hellos)
    send_halo(0)
    for load in loads[3:]:
        load.wait()

    ct_all = cot[...].astype(F32) * maskb[...]
    gb_all = (ct_all * scale[...].reshape(1, 1, C)).reshape(CELLS, C)
    bcot_s[...] = gb_all.astype(BF16)
    sums[2] = jnp.sum(gb_all.reshape(CELLS // 8, 8, C), axis=0)
    for t in range(HID // 256):
        wide = slice(256 * t, 256 * t + 256)
        ghid_s[:, wide] = dot(bcot_s[...], w_out[:, wide])

    @pl.loop(3, 3 + ROWS, unroll=4)
    def _(r):
        shift_some(r, inner)

    @pl.loop(1, ROWS // 4 - 1)
    def _(i):
        conv_inner(4 * i)

    take_halo(0, pad)

    @pl.loop(3, 3 + ROWS, unroll=4)
    def _(r):
        shift_some(r, lambda b, h: not inner(b, h))

    for q in range(3):
        shift_some(q, lambda b, h: True)
        shift_some(ROWS + 3 + q, lambda b, h: True)
    conv_inner(0)
    conv_inner(ROWS - 4)

    block = ROWS
    cells = block * COLS

    @pl.loop(0, ROWS // block)
    def _(blk):
        r0 = blk * block
        here = pl.ds(pl.multiple_of(r0 * COLS, cells), cells)
        mixed = jnp.concatenate(
            [conv_outer(r0 + 4 * i) for i in range(block // 4)],
            axis=0,
        )
        average = jnp.sum(mixed, axis=1, keepdims=True) * (1.0 / C)
        centred = mixed - average
        variance = jnp.sum(centred * centred, axis=1, keepdims=True) * (1.0 / C)
        inv_std = lax.rsqrt(variance + EPSILON)
        unit = centred * inv_std
        normed = (unit * gain[...] + nbias[...]).astype(BF16)
        normed_s[here, :] = normed
        pre = dot(normed, w_in[...]) + b_hid[...].reshape(HID)
        square = pre * pre
        t = jnp.tanh(GELU_A * pre * (1.0 + GELU_B * square))
        half = 0.5 * (1.0 + t)
        hidden = (pre * half).astype(BF16)
        hidden_s[here, :] = hidden
        slope = half + pre * (0.5 * GELU_A) * (1.0 - t * t) * (1.0 + 3.0 * GELU_B * square)
        branch = dot(hidden, w_out[...], ((1,), (1,))) + b_out[...]
        rows_here = pl.ds(r0, block)
        sea_w = maskb[rows_here].reshape(cells, C)
        st = state[rows_here].astype(F32).reshape(cells, C)
        ct = cot[rows_here].astype(F32).reshape(cells, C) * sea_w
        block_out[rows_here] = (
            (sea_w * (st + scale[...] * branch)).astype(BF16).reshape(block, COLS, C)
        )
        grad_pre = ghid_s[here, :] * slope
        precot = grad_pre.astype(BF16)
        precot_s[here, :] = precot
        grad_normed = dot(precot, w_in[...], ((1,), (1,)))
        grad_unit = grad_normed * gain[...]
        mean_a = jnp.sum(grad_unit, axis=1, keepdims=True) * (1.0 / C)
        mean_b = jnp.sum(grad_unit * unit, axis=1, keepdims=True) * (1.0 / C)
        grad_mixed = inv_std * (grad_unit - mean_a - unit * mean_b)
        mcot = grad_mixed.astype(BF16)
        own_s[1, rows_here] = mcot.reshape(block, COLS, C)
        padq[pl.ds(3 + r0, block), 8:24, :] = mcot.astype(F32).reshape(block, COLS, C)

        def fold8(v):
            return jnp.sum(v.reshape(cells // 8, 8, v.shape[1]), axis=0)

        sums[0] += fold8(grad_normed * unit)
        sums[1] += fold8(grad_normed)
        sums[3] += fold8(ct * branch)
        sumh[...] += fold8(grad_pre)

    pick_halo(1)
    send_halo(1)
    block_store = pltpu.make_async_copy(block_out, block_h, store_s.at[0])
    block_store.start()

    for t in range(HID // 256):
        wide = slice(256 * t, 256 * t + 256)
        g_in = dot(normed_s[...], precot_s[:, wide], ((0,), (0,)))
        g_out = dot(bcot_s[...], hidden_s[:, wide], ((0,), (0,)))
        for j in range(2):
            to = slice((2 * t + j) * C, (2 * t + j + 1) * C)
            wbuf[0, to, :] = g_in[:, 128 * j : 128 * j + 128]
            wbuf[1, to, :] = g_out[:, 128 * j : 128 * j + 128]

    def to_pair(i, rows):
        return remote("pair", wbuf.at[1 - core, rows], wrecv.at[rows], core_s.at[i], core_r.at[i], pair)

    pair_w = to_pair(0, pl.ds(0, WROWS))
    pair_w.start()

    def kernel_grad(b):
        def step(i, accs):
            r0 = i * 4
            m = padq[pl.ds(3 + r0, 4), 8:24, :].reshape(4, 2, 8, C)
            win = shifted[b, pl.ds(r0, 10)]
            return tuple(
                accs[a] + jnp.sum((m * win[a : a + 4]).reshape(8, 8, C), axis=0)
                for a in range(7)
            )

        accs = lax.fori_loop(0, ROWS // 4, step, tuple(jnp.zeros((8, C), F32) for _ in range(7)))
        for a in range(7):
            small[a * 7 + b : a * 7 + b + 1, 0:C] = jnp.sum(accs[a], axis=0, keepdims=True)

    for b in range(3):
        kernel_grad(b)

    def group_copy(k, sender):
        return remote("group", pay.at[k], xrecv.at[sender], xs.at[k], xr.at[sender], in_group(k))

    def rest_copy(k, sender):
        return remote("group", payx.at[k], xrecvx.at[sender], xsx.at[k], xrx.at[sender], in_group(k))

    pair_w.wait()

    def add_pair(k):
        rows = pl.ds(pl.multiple_of(k * mrows, 32), mrows)
        both = wbuf[core, rows, :] + wrecv[rows, :]
        psum[rows, :] = both
        pay[k] = both.astype(BF16)

    add_pair(me)

    def far(i, n, first):
        return 1 + lax.rem(i + first, n - 1)

    @pl.loop(0, size - 1)
    def _(i):
        k = lax.rem(me + far(i, size, size * 5 // 8 - 1), size)
        add_pair(k)
        group_copy(k, me).start()

    for b in range(3, 7):
        kernel_grad(b)
    for i in range(4):
        small[49 + i : 50 + i, 0:C] = jnp.sum(sums[i], axis=0, keepdims=True)
    hid_row = jnp.sum(sumh[...], axis=0, keepdims=True)
    for i in range(3):
        small[53 + i : 54 + i, :] = hid_row[:, 256 * i : 256 * i + 256]
    wbuf[0, WROWS:, :] = small[:, 0:128]
    wbuf[1, WROWS:, :] = small[:, 128:256]
    pair_s = to_pair(1, pl.ds(WROWS, SROWS))
    pair_s.start()

    pair_s.wait()
    rest_w = wbuf[core, MAIN:WROWS, :] + wrecv[MAIN:WROWS, :]
    both = wbuf[core, WROWS:, :] + wrecv[WROWS:, :]
    high = both.astype(BF16).astype(F32)
    other = jnp.concatenate([rest_w, high, both - high], axis=0)
    for i in range((TOT - MAIN) // size):
        extra[pl.ds(i, size, stride=erows), :] = other[i * size : (i + 1) * size]
    payx[...] = extra[...].reshape(size, erows, 128).astype(BF16)

    @pl.loop(0, size - 1)
    def _(i):
        k = lax.rem(me + far(i, size, size * 5 // 8 - 1), size)
        rest_copy(k, me).start()

    def halves(v):
        first = (WROWS - MAIN) // size
        count = SROWS // size
        end = v.shape[0]
        row = lax.broadcasted_iota(jnp.int32, v.shape, 0) - mrows
        whole = v + pltpu.roll(v, end - count, 0)
        top = whole.astype(BF16).astype(F32)
        low = pltpu.roll(whole - top, count, 0)
        is_high = (row >= first) & (row < first + count)
        is_low = (row >= first + count) & (row < first + 2 * count)
        return jnp.where(is_high, top, jnp.where(is_low, low, v)).astype(BF16)

    @pl.loop(1, size)
    def _(d):
        k = lax.rem(me + d, size)
        group_copy(k, k).wait()

    def add_main(d, acc):
        return acc + xrecv[lax.rem(me + d, size)].astype(F32)

    def add_rest(d, acc):
        return acc + xrecvx[lax.rem(me + d, size)].astype(F32)

    mine = psum[pl.ds(pl.multiple_of(me * mrows, 32), mrows), :]
    mine = lax.fori_loop(1, size, add_main, mine)

    @pl.loop(1, size)
    def _(d):
        k = lax.rem(me + d, size)
        rest_copy(k, k).wait()

    minex = extra[pl.ds(pl.multiple_of(me * erows, 16), erows), :]
    minex = lax.fori_loop(1, size, add_rest, minex)
    zslot[zi] = halves(jnp.concatenate([mine, minex], axis=0))

    def z_copy(k, sender):
        return remote("z", zslot.at[sender], zslot.at[sender], zs.at[k], zr.at[sender], in_z(k))

    @pl.loop(0, nz - 1)
    def _(i):
        z_copy(lax.rem(zi + far(i, nz, nz // 2 - 1), nz), zi).start()

    @pl.loop(1, nz)
    def _(d):
        k = lax.rem(zi + d, nz)
        z_copy(k, k).wait()

    whole = zslot[0].astype(F32)
    for k in range(1, nz):
        whole = whole + zslot[k].astype(F32)
    abuf[me] = halves(whole)

    def back_copy(owner, k):
        return remote("back", abuf.at[owner], abuf.at[owner], xas.at[k], xar.at[owner], in_group(k))

    @pl.loop(0, size - 1)
    def _(i):
        back_copy(me, lax.rem(me + far(i, size, size * 5 // 8 - 1), size)).start()

    def last_copy(k):
        return remote("last", abuf.at[k], fin.at[k], ls.at[k], lr.at[k], pair)

    last_copy(me).start()

    take_halo(1, padq)
    shift(padq, shiftq)

    @pl.loop(0, ROWS // 2)
    def _(i):
        rows_here = pl.ds(i * 2, 2)
        grad = conv_rows(shiftq, i * 2, 2, True).reshape(2, COLS, C)
        grad_state[rows_here] = (
            maskb[rows_here] * (cot[rows_here].astype(F32) + grad)
        ).astype(BF16)

    @pl.when(is_top)
    def _():
        first = ROWS - 4
        acc = conv_rows(shiftq, first, 4, True)
        parts = [acc[i] for i in range(4)]
        for i in range(1, 4):
            for a in range(7 - i, 7):
                for b in range(7):
                    change = taps[a * 7 + b] - taps[48 - a * 7 - b]
                    parts[i] = parts[i] + shiftq[b, first + i + a] * change
        for i in range(1, 4):
            grad_state[first + i] = (
                maskb[first + i] * (cot[first + i].astype(F32) + parts[i].reshape(COLS, C))
            ).astype(BF16)

    grad_store = pltpu.make_async_copy(grad_state, grad_h, store_s.at[1])
    grad_store.start()

    @pl.loop(1, size)
    def _(d):
        k = lax.rem(me + d, size)
        back_copy(k, k).wait()
        last_copy(k).start()

    own_store = pltpu.make_async_copy(abuf, total.at[core], store_s.at[2])
    own_store.start()

    @pl.loop(0, size)
    def _(k):
        last_copy(k).wait()

    fin_store = pltpu.make_async_copy(fin, total.at[1 - core], store_s.at[3])
    fin_store.start()
    for store in (block_store, grad_store, own_store, fin_store):
        store.wait()


def finish_kernel(
    factor, size, mrows, erows, total_h, block_h, grad_h,
    block_out, grad_out, gk, gg, gb, gw_in, gbh, gw_out, gbo, gls, total, extra, sem,
):
    moves = [
        pltpu.make_async_copy(src, dst, sem.at[i])
        for i, (src, dst) in enumerate(
            ((total_h, total), (block_h, block_out), (grad_h, grad_out))
        )
    ]
    for move in moves:
        move.start()
    moves[0].wait()
    small = []
    for c, gw in ((0, gw_in), (1, gw_out)):
        rows = total[c, :, 0:mrows, :].reshape(MAIN, 128).astype(F32) * factor
        extra[...] = total[c, :, mrows:, :].reshape(size * erows, 128).astype(F32) * factor
        rest = [extra[pl.ds(i, size, stride=erows), :] for i in range((TOT - MAIN) // size)]
        rows = jnp.concatenate([rows] + rest, axis=0)
        for t in range(HID // 128):
            gw[:, 128 * t : 128 * t + 128] = rows[t * C : (t + 1) * C]
        small.append(rows[WROWS : WROWS + SROWS] + rows[WROWS + SROWS :])
    near, far = small
    for a in range(7):
        gk[a, :, 0:128] = near[7 * a : 7 * a + 7]
        gk[a, :, 128:C] = far[7 * a : 7 * a + 7, 0 : C - 128]
    for i, out in enumerate((gg, gb, gbo, gls)):
        out[:, 0:128] = near[49 + i : 50 + i]
        out[:, 128:C] = far[49 + i : 50 + i, 0 : C - 128]
    for i in range(3):
        gbh[256 * i : 256 * i + 128] = near[53 + i]
        gbh[256 * i + 128 : 256 * i + 256] = far[53 + i]
    for move in moves[1:]:
        move.wait()


def on_device(
    nlon,
    nlat,
    state,
    land_mask,
    cotangent,
    kernel,
    norm_gain,
    norm_bias,
    weight_in,
    bias_hidden,
    weight_out,
    bias_out,
    layer_scale,
):
    size, nz, mrows, erows = shares(nlon, nlat)
    hbm = pl.BlockSpec(memory_space=pltpu.HBM)
    vmem = pl.BlockSpec(memory_space=pltpu.VMEM)
    dma = pltpu.SemaphoreType.DMA
    row = lambda v: v.reshape(1, -1)
    block, grad, total = pl.pallas_call(
        functools.partial(main_kernel, nlon, nlat),
        out_shape=(
            jax.ShapeDtypeStruct((ROWS, COLS, C), BF16),
            jax.ShapeDtypeStruct((ROWS, COLS, C), BF16),
            jax.ShapeDtypeStruct((2, size, mrows + erows, 128), BF16),
        ),
        in_specs=[hbm] * 11,
        out_specs=(hbm,) * 3,
        scratch_shapes=[
            pltpu.VMEM((ROWS, COLS, C), BF16),
            pltpu.VMEM((ROWS, COLS, C), BF16),
            pltpu.VMEM((ROWS, COLS, C), BF16),
            pltpu.VMEM((COLS, ROWS), jnp.int32),
            pltpu.VMEM((ROWS, COLS, C), BF16),
            pltpu.VMEM((7, 7, C), BF16),
            pltpu.VMEM((1, C), F32),
            pltpu.VMEM((1, C), F32),
            pltpu.VMEM((C, HID), BF16),
            pltpu.VMEM((HID,), F32),
            pltpu.VMEM((C, HID), BF16),
            pltpu.VMEM((1, C), F32),
            pltpu.VMEM((1, C), F32),
            pltpu.VMEM((PADR, WIDE, C), F32),
            pltpu.VMEM((7, PADR, 2, 8, C), F32),
            pltpu.VMEM((PADR, WIDE, C), F32),
            pltpu.VMEM((7, PADR, 2, 8, C), F32),
            pltpu.VMEM((49, 8, C), F32),
            pltpu.VMEM((ROWS, COLS, C), F32),
            pltpu.VMEM((ROWS, 2, 8, C), F32),
            pltpu.VMEM((CELLS, HID), F32),
            pltpu.VMEM((CELLS, C), BF16),
            pltpu.VMEM((CELLS, HID), BF16),
            pltpu.VMEM((CELLS, HID), BF16),
            pltpu.VMEM((CELLS, C), BF16),
            pltpu.VMEM((2, ROWS, COLS, C), BF16),
            pltpu.VMEM((4, 8, C), F32),
            pltpu.VMEM((8, HID), F32),
            pltpu.VMEM((SROWS, 256), F32),
            pltpu.VMEM((2, 2, 96, C), BF16),
            pltpu.VMEM((2, 4, 16, C), BF16),
            pltpu.VMEM((2, 2, 96, C), BF16),
            pltpu.VMEM((2, 2, 5, 16, C), BF16),
            pltpu.VMEM((2, WROWS + SROWS, 128), F32),
            pltpu.VMEM((WROWS + SROWS, 128), F32),
            pltpu.VMEM((MAIN, 128), F32),
            pltpu.VMEM((size * erows, 128), F32),
            pltpu.VMEM((size, mrows, 128), BF16),
            pltpu.VMEM((size, mrows, 128), BF16),
            pltpu.VMEM((size, erows, 128), BF16),
            pltpu.VMEM((size, erows, 128), BF16),
            pltpu.VMEM((nz, mrows + erows, 128), BF16),
            pltpu.VMEM((size, mrows + erows, 128), BF16),
            pltpu.VMEM((size, mrows + erows, 128), BF16),
            dma((11,)),
            dma((4,)),
            dma((2, 8)),
            dma((2, 8)),
            dma((2,)),
            dma((2,)),
            dma((size,)),
            dma((size,)),
            dma((size,)),
            dma((size,)),
            dma((nz,)),
            dma((nz,)),
            dma((size,)),
            dma((size,)),
            dma((size,)),
            dma((size,)),
        ],
        compiler_params=pltpu.CompilerParams(
            collective_id=0, has_side_effects=True, vmem_limit_bytes=56 * 1024 * 1024
        ),
        name="block",
    )(
        state,
        land_mask.T,
        cotangent,
        kernel,
        row(norm_gain),
        row(norm_bias),
        weight_in,
        bias_hidden,
        weight_out.T,
        row(bias_out),
        row(layer_scale),
    )
    factor = 1.0 / math.sqrt(ROWS * nlat * COLS * nlon)
    shape = lambda *s: jax.ShapeDtypeStruct(s, F32)
    outs = pl.pallas_call(
        functools.partial(finish_kernel, factor, size, mrows, erows),
        out_shape=(
            jax.ShapeDtypeStruct((ROWS, COLS, C), BF16),
            jax.ShapeDtypeStruct((ROWS, COLS, C), BF16),
            shape(7, 7, C),
            shape(1, C),
            shape(1, C),
            shape(C, HID),
            shape(HID),
            shape(C, HID),
            shape(1, C),
            shape(1, C),
        ),
        in_specs=[hbm] * 3,
        out_specs=(vmem,) * 10,
        scratch_shapes=[
            pltpu.VMEM((2, size, mrows + erows, 128), BF16),
            pltpu.VMEM((size * erows, 128), F32),
            dma((3,)),
        ],
        compiler_params=pltpu.CompilerParams(vmem_limit_bytes=56 * 1024 * 1024),
        name="finish",
    )(total, block, grad)
    outs = [o.reshape(-1) if o.shape[0] == 1 else o for o in outs]
    outs[7] = outs[7].T
    return tuple(outs)


def solution(mesh):
    cells, plane, whole = P("lat", "lon", None), P("lat", "lon"), P()
    return jax.shard_map(
        functools.partial(on_device, mesh.shape["lon"], mesh.shape["lat"]),
        mesh=mesh,
        in_specs=(cells, plane, cells) + (whole,) * 8,
        out_specs=(cells, cells) + (whole,) * 8,
        check_vma=False,
    )
```
